256 devices in a mesh: grp: 16 (over z, core), row: 16 (over y, x).
Axes of the slice: x: 4, y: 4, z: 8, core: 2. Of those that a mesh axis runs over, the one named last changes fastest.
Arguments:
- iterate: bfloat16 [32768, 4096], P(('grp', 'row')), parts along dimension 0
- block_matrix: int32 [256], P('grp'), parts along dimension 0, may hold values from 0 to 3, as said below
Outputs:
- update: bfloat16 [32768, 4096], P(('grp', 'row')), parts along dimension 0
The draws below stay inside these ranges and needn't reach their ends.
There are 16 independent parts, one for each index of `grp`. The reference program is written for one: setup_inputs(seed, part) draws one part's arguments, and reference() takes and returns one part's arrays. A program takes and returns all parts, laid end to end along the dimension named above; each array names one. Nothing has to cross between parts.
Inputs may be any that keep to these rules, and one draw needn't show every extreme that they name: `block_matrix`: every row range holds exactly 4 blocks, in any order.
All inputs are finite; a program needn't handle non-finite values.
Results may differ from the reference program's by a relative error of at most 0.0066.
Values may be sent and summed in bfloat16 or wider, within the bound.
A program may use at most 192 MiB of HBM per device.

```python
import math
import jax
import jax.numpy as jnp
from jax import lax

ROWS = 2048
COLS = 4096
KV_ROWS = 512
HALF = 2048
BLK = 128
BLOCKS = 16
MATS = 4


def draw_block_matrix(key, part):
    key = jax.random.fold_in(key, 11)
    order = jax.random.permutation(key, BLOCKS).astype(jnp.int32)
    return (order // (KV_ROWS // BLK)).astype(jnp.int32)


def draw_iterate(key, part):
    key = jax.random.fold_in(key, 7)
    key_base, key_rows, key_cols = jax.random.split(key, 3)
    level = 0.7 / math.sqrt(HALF)
    base = jnp.clip(jax.random.normal(key_base, (ROWS, COLS), jnp.float32), -6.0, 6.0)
    row_scale = jnp.exp(jax.random.uniform(key_rows, (ROWS, 1), jnp.float32, math.log(0.6), math.log(1.5)))
    col_scale = jnp.exp(jax.random.uniform(key_cols, (1, COLS), jnp.float32, math.log(0.6), math.log(1.5)))
    return (level * base * row_scale * col_scale).astype(jnp.bfloat16)


def setup_inputs(seed: int = 0, part: int = 0) -> dict:
    seeds = jax.random.split(jax.random.key(seed), 3)
    part_splits = jax.random.split(jax.random.fold_in(seeds[2], part), 3)
    return {
        "iterate": draw_iterate(jax.random.fold_in(jax.random.fold_in(seeds[2], part), 71), part),
        "block_matrix": draw_block_matrix(jax.random.fold_in(jax.random.fold_in(seeds[2], part), 71), part),
    }


A_COEF = 3.4445
B_COEF = -4.775
C_COEF = 2.0315
eps = 1e-06

def reference(iterate, block_matrix):
    owner = jnp.repeat(block_matrix, BLK).astype(jnp.int32)
    same_matrix = owner[:, None] == owner[None, :]
    halves = [iterate[:, :HALF], iterate[:, HALF:]]
    matrix_ids = jnp.arange(MATS, dtype=jnp.int32)
    onehot = (owner[:, None] == matrix_ids[None, :]).astype(jnp.float32)
    counts = lax.optimization_barrier(jnp.sum(onehot, axis=0)) * HALF
    own_count = lax.optimization_barrier(jnp.sum(onehot * counts[None, :], axis=1))
    outputs = []
    for h in range(2):
        part = jnp.dot(halves[h], halves[h].T, preferred_element_type=jnp.float32)
        gram = jnp.where(same_matrix, part, jnp.zeros_like(part)).astype(jnp.bfloat16)
        square = jnp.dot(gram, gram, preferred_element_type=jnp.float32)
        poly = (B_COEF * gram.astype(jnp.float32) + C_COEF * square).astype(jnp.bfloat16)
        raw = A_COEF * halves[h].astype(jnp.float32) + jnp.dot(poly, halves[h], preferred_element_type=jnp.float32)
        energy = lax.optimization_barrier(jnp.sum(onehot * lax.optimization_barrier(jnp.sum(raw * raw, axis=1))[:, None], axis=0))
        own_energy = lax.optimization_barrier(jnp.sum(onehot * energy[None, :], axis=1))
        factor = lax.rsqrt(own_energy / own_count + eps)
        outputs.append(raw * factor[:, None])
    return jnp.concatenate(outputs, axis=1).astype(jnp.bfloat16)
```

```python
import functools

import jax
import jax.numpy as jnp
from jax import lax
from jax.experimental import pallas as pl
from jax.experimental.pallas import tpu as pltpu
from jax.sharding import PartitionSpec as P

BLK = 128
SIDE = 4
DEVS = SIDE * SIDE
SUB = 256
KV_ROWS = 512
HALF = 2048
MESH = pl.DeviceIdType.MESH

A_COEF = 3.4445
B_COEF = -4.775
C_COEF = 2.0315
eps = 1e-06
F32 = jnp.float32
BF16 = jnp.bfloat16


def kernel(
    owner_ref, x_ref, out_ref,
    in_sub, in_sorted, mat, part_out, part_in, new_out, new_in, out_blocks,
    local_sem, s1, r1, s2, r2, s3, r3, s4, r4, s5, r5,
):
    group = lax.axis_index("grp")
    me = lax.axis_index("row")
    turn = lax.rem(group, 2)
    y, x = me // SIDE, lax.rem(me, SIDE)
    a = y + turn * (x - y)
    b = x + turn * (y - x)
    step_a = SIDE - (SIDE - 1) * turn
    step_b = 1 + (SIDE - 1) * turn

    def device(a_, b_):
        return a_ * step_a + b_ * step_b

    def shift(v, d):
        return lax.rem(v + d, SIDE)

    hops = [(da, db) for da in range(SIDE) for db in range(SIDE) if (da, db) != (0, 0)]
    hops.sort(key=lambda h: -(min(h[0], SIDE - h[0]) + min(h[1], SIDE - h[1])))
    peers = [(shift(a, da), shift(b, db)) for da, db in hops]

    def columns(a_, b_):
        return pl.ds(pl.multiple_of((a_ * SIDE + b_) * SUB, SUB), SUB)

    barrier = pltpu.get_barrier_semaphore()
    for pa, pb in peers:
        pl.semaphore_signal(barrier, inc=1, device_id=(group, device(pa, pb)), device_id_type=MESH)
    pl.semaphore_wait(barrier, DEVS - 1)

    def to_sub(pa, pb):
        d = device(pa, pb)
        return pltpu.make_async_remote_copy(
            src_ref=x_ref.at[:, columns(pa, pb)], dst_ref=in_sub.at[me],
            send_sem=s1.at[d], recv_sem=r1.at[me], device_id=(group, d), device_id_type=MESH,
        )

    def from_sub(pa, pb):
        d = device(pa, pb)
        return pltpu.make_async_remote_copy(
            src_ref=x_ref.at[:, columns(pa, pb)], dst_ref=in_sub.at[d],
            send_sem=s1.at[d], recv_sem=r1.at[d], device_id=(group, d), device_id_type=MESH,
        )

    for pa, pb in peers:
        to_sub(pa, pb).start()
    own = pltpu.make_async_copy(x_ref.at[:, columns(a, b)], in_sub.at[me], local_sem.at[0])
    own.start()

    owners = [owner_ref[r] for r in range(DEVS)]
    places = []
    for r in range(DEVS):
        p = owners[r] * SIDE
        for q in range(r):
            p = p + jnp.where(owners[q] == owners[r], 1, 0)
        places.append(p)
    order = []
    for k in range(DEVS):
        o = jnp.int32(0)
        for r in range(1, DEVS):
            o = o + jnp.where(places[r] == k, r, 0)
        order.append(o)

    own.wait()
    for pa, pb in peers:
        from_sub(pa, pb).wait_recv()

    def to_mat(m):
        d = device(a, m)
        return pltpu.make_async_remote_copy(
            src_ref=in_sorted.at[m], dst_ref=mat.at[b],
            send_sem=s2.at[m], recv_sem=r2.at[b], device_id=(group, d), device_id_type=MESH,
        )

    def from_mat(q):
        d = device(a, q)
        return pltpu.make_async_remote_copy(
            src_ref=in_sorted.at[q], dst_ref=mat.at[q],
            send_sem=s2.at[q], recv_sem=r2.at[q], device_id=(group, d), device_id_type=MESH,
        )

    for m in range(SIDE):
        for i in range(SIDE):
            in_sorted[m, i * BLK:(i + 1) * BLK, :] = in_sub[order[m * SIDE + i]]
    for db in (2, 1, 3):
        to_mat(shift(b, db)).start()
    mat[b] = in_sorted[b]
    for db in (1, 3, 2):
        from_mat(shift(b, db)).wait_recv()

    part = jnp.zeros((KV_ROWS, KV_ROWS), F32)
    for q in range(SIDE):
        part = part + lax.dot_general(
            mat[q], mat[q], (((1,), (1,)), ((), ())), preferred_element_type=F32
        )
    part_out[...] = part.astype(BF16)
    partner = a + 1 - 2 * lax.rem(a, 2)
    swap = pltpu.make_async_remote_copy(
        src_ref=part_out, dst_ref=part_in, send_sem=s3, recv_sem=r3,
        device_id=(group, device(partner, b)), device_id_type=MESH,
    )
    swap.start()
    swap.wait_recv()
    gram = (part + part_in[...].astype(F32)).astype(BF16)
    square = jnp.dot(gram, gram, preferred_element_type=F32)
    gram32 = gram.astype(F32)
    poly = (B_COEF * gram32 + C_COEF * square).astype(BF16)
    poly32 = poly.astype(F32)

    turned = jnp.dot(poly, gram, preferred_element_type=F32)
    diagonal = lax.broadcasted_iota(jnp.int32, (KV_ROWS, KV_ROWS), 0) == lax.broadcasted_iota(
        jnp.int32, (KV_ROWS, KV_ROWS), 1
    )
    terms = (
        jnp.where(diagonal, (A_COEF * A_COEF) * gram32, 0.0)
        + (2 * A_COEF) * (poly32 * gram32)
        + turned * poly32
    )
    energy = jnp.sum(jnp.sum(terms, axis=0, keepdims=True), axis=1, keepdims=True)
    factor = lax.rsqrt(energy / (KV_ROWS * HALF) + eps)

    def to_new(q):
        return pltpu.make_async_remote_copy(
            src_ref=new_out.at[q], dst_ref=new_in.at[pl.ds(b * SIDE, SIDE)],
            send_sem=s4.at[q], recv_sem=r4.at[b], device_id=(group, device(a, q)), device_id_type=MESH,
        )

    def from_new(q):
        return pltpu.make_async_remote_copy(
            src_ref=new_out.at[q], dst_ref=new_in.at[pl.ds(q * SIDE, SIDE)],
            send_sem=s4.at[q], recv_sem=r4.at[q], device_id=(group, device(a, q)), device_id_type=MESH,
        )

    def update(q):
        block = mat[q]
        raw = A_COEF * block.astype(F32) + jnp.dot(poly, block, preferred_element_type=F32)
        return (raw * factor).astype(BF16).reshape(SIDE, BLK, SUB)

    for db in (2, 1, 3):
        q = shift(b, db)
        new_out[q] = update(q)
        to_new(q).start()
    new_in[pl.ds(b * SIDE, SIDE)] = update(b)
    for db in (1, 3, 2):
        from_new(shift(b, db)).wait_recv()

    def to_out(pa, pb):
        d = device(pa, pb)
        return pltpu.make_async_remote_copy(
            src_ref=out_blocks.at[d], dst_ref=out_ref.at[:, columns(a, b)],
            send_sem=s5.at[d], recv_sem=r5.at[me], device_id=(group, d), device_id_type=MESH,
        )

    def from_out(pa, pb):
        d = device(pa, pb)
        return pltpu.make_async_remote_copy(
            src_ref=out_blocks.at[d], dst_ref=out_ref.at[:, columns(pa, pb)],
            send_sem=s5.at[d], recv_sem=r5.at[d], device_id=(group, d), device_id_type=MESH,
        )

    for r in range(DEVS):
        out_blocks[r] = new_in[places[r]]
    for pa, pb in peers:
        to_out(pa, pb).start()
    own = pltpu.make_async_copy(out_blocks.at[me], out_ref.at[:, columns(a, b)], local_sem.at[1])
    own.start()
    own.wait()
    for pa, pb in peers:
        from_out(pa, pb).wait_recv()

    for pa, pb in peers:
        to_sub(pa, pb).wait_send()
        to_out(pa, pb).wait_send()
    for db in (1, 2, 3):
        to_mat(shift(b, db)).wait_send()
        to_new(shift(b, db)).wait_send()
    swap.wait_send()


def shards(iterate, block_matrix):
    dma = pltpu.SemaphoreType.DMA
    return pl.pallas_call(
        kernel,
        out_shape=jax.ShapeDtypeStruct(iterate.shape, BF16),
        in_specs=[pl.BlockSpec(memory_space=pltpu.SMEM), pl.BlockSpec(memory_space=pl.ANY)],
        out_specs=pl.BlockSpec(memory_space=pl.ANY),
        scratch_shapes=[
            pltpu.VMEM((DEVS, BLK, SUB), BF16),
            pltpu.VMEM((SIDE, KV_ROWS, SUB), BF16),
            pltpu.VMEM((SIDE, KV_ROWS, SUB), BF16),
            pltpu.VMEM((KV_ROWS, KV_ROWS), BF16),
            pltpu.VMEM((KV_ROWS, KV_ROWS), BF16),
            pltpu.VMEM((SIDE, SIDE, BLK, SUB), BF16),
            pltpu.VMEM((DEVS, BLK, SUB), BF16),
            pltpu.VMEM((DEVS, BLK, SUB), BF16),
            dma((2,)),
            dma((DEVS,)), dma((DEVS,)),
            dma((SIDE,)), dma((SIDE,)),
            dma, dma,
            dma((SIDE,)), dma((SIDE,)),
            dma((DEVS,)), dma((DEVS,)),
        ],
        compiler_params=pltpu.CompilerParams(
            collective_id=0, has_side_effects=True, vmem_limit_bytes=48 * 1024 * 1024
        ),
        cost_estimate=pl.CostEstimate(flops=1_900_000_000, bytes_accessed=4_194_304, transcendentals=0),
    )(block_matrix, iterate)


def solution(mesh):
    return jax.shard_map(
        shards,
        mesh=mesh,
        in_specs=(P(("grp", "row"), None), P("grp")),
        out_specs=P(("grp", "row"), None),
        check_vma=False,
    )
```

```python
import functools

import jax
import jax.numpy as jnp
from jax import lax
from jax.experimental import pallas as pl
from jax.experimental.pallas import tpu as pltpu
from jax.sharding import PartitionSpec as P

BLK = 128
SIDE = 4
DEVS = SIDE * SIDE
SUB = 256
KV_ROWS = 512
HALF = 2048
MESH = pl.DeviceIdType.MESH

A_COEF = 3.4445
B_COEF = -4.775
C_COEF = 2.0315
eps = 1e-06
F32 = jnp.float32
BF16 = jnp.bfloat16


def kernel(
    owner_hbm, x_ref, out_ref,
    owner_ref, in_sub, in_sorted, mat, part_out, part_in, gram_ref, new_out, new_in, out_blocks,
    local_sem, gate, s1, r1, s2, r2, s3, r3, s4, r4, s5, r5,
):
    group = lax.axis_index("grp")
    me = lax.axis_index("row")
    turn = lax.rem(group, 2)
    y, x = me // SIDE, lax.rem(me, SIDE)
    a = y + turn * (x - y)
    b = x + turn * (y - x)
    step_a = SIDE - (SIDE - 1) * turn
    step_b = 1 + (SIDE - 1) * turn

    def device(a_, b_):
        return a_ * step_a + b_ * step_b

    def shift(v, d):
        return lax.rem(v + d, SIDE)

    near = [(shift(a, d), b) for d in (2, 1, 3)] + [(a, shift(b, d)) for d in (2, 1, 3)]
    far = [(shift(a, da), shift(b, db)) for da in (2, 1, 3) for db in (2, 1, 3)]
    peers = far + near

    def columns(a_, b_):
        return pl.ds(pl.multiple_of((a_ * SIDE + b_) * SUB, SUB), SUB)

    fetch = pltpu.make_async_copy(owner_hbm, owner_ref, local_sem.at[2])
    fetch.start()
    barrier = pltpu.get_barrier_semaphore()
    for pa, pb in near:
        pl.semaphore_signal(barrier, inc=1, device_id=(group, device(pa, pb)), device_id_type=MESH)
    pl.semaphore_wait(barrier, len(near))
    for pa, pb in near:
        if pb is b:
            pl.semaphore_signal(gate, inc=1, device_id=(group, device(pa, pb)), device_id_type=MESH)

    def to_sub(pa, pb):
        d = device(pa, pb)
        return pltpu.make_async_remote_copy(
            src_ref=x_ref.at[:, columns(pa, pb)], dst_ref=in_sub.at[me],
            send_sem=s1.at[d], recv_sem=r1.at[me], device_id=(group, d), device_id_type=MESH,
        )

    def from_sub(pa, pb):
        d = device(pa, pb)
        return pltpu.make_async_remote_copy(
            src_ref=x_ref.at[:, columns(pa, pb)], dst_ref=in_sub.at[d],
            send_sem=s1.at[d], recv_sem=r1.at[d], device_id=(group, d), device_id_type=MESH,
        )

    for pa, pb in near:
        to_sub(pa, pb).start()
    pl.semaphore_wait(gate, SIDE - 1)
    for pa, pb in far:
        to_sub(pa, pb).start()
    own = pltpu.make_async_copy(x_ref.at[:, columns(a, b)], in_sub.at[me], local_sem.at[0])
    own.start()

    fetch.wait()
    owners = [owner_ref[r] for r in range(DEVS)]
    places = []
    for r in range(DEVS):
        p = owners[r] * SIDE
        for q in range(r):
            p = p + jnp.where(owners[q] == owners[r], 1, 0)
        places.append(p)
    order = []
    for k in range(DEVS):
        o = jnp.int32(0)
        for r in range(1, DEVS):
            o = o + jnp.where(places[r] == k, r, 0)
        order.append(o)

    own.wait()
    for pa, pb in peers:
        from_sub(pa, pb).wait_recv()

    def to_mat(m):
        d = device(a, m)
        return pltpu.make_async_remote_copy(
            src_ref=in_sorted.at[m], dst_ref=mat.at[b],
            send_sem=s2.at[m], recv_sem=r2.at[b], device_id=(group, d), device_id_type=MESH,
        )

    def from_mat(q):
        d = device(a, q)
        return pltpu.make_async_remote_copy(
            src_ref=in_sorted.at[q], dst_ref=mat.at[q],
            send_sem=s2.at[q], recv_sem=r2.at[q], device_id=(group, d), device_id_type=MESH,
        )

    for m in range(SIDE):
        for i in range(SIDE):
            in_sorted[m, i * BLK:(i + 1) * BLK, :] = in_sub[order[m * SIDE + i]]
    for db in (2, 1, 3):
        to_mat(shift(b, db)).start()
    mat[b] = in_sorted[b]

    def product(q):
        block = mat[q]
        return [
            lax.dot_general(
                block[i * BLK:(i + 1) * BLK, :], block[i * BLK:, :],
                (((1,), (1,)), ((), ())), preferred_element_type=F32,
            )
            for i in range(SIDE)
        ]

    part = product(b)
    for db in (1, 3, 2):
        q = shift(b, db)
        from_mat(q).wait_recv()
        part = [p + new for p, new in zip(part, product(q))]
    starts = [0, 4 * BLK, 7 * BLK, 9 * BLK, 10 * BLK]
    for i in range(SIDE):
        part_out[:, starts[i]:starts[i + 1]] = part[i].astype(BF16)
    partner = a + 1 - 2 * lax.rem(a, 2)
    swap = pltpu.make_async_remote_copy(
        src_ref=part_out, dst_ref=part_in, send_sem=s3, recv_sem=r3,
        device_id=(group, device(partner, b)), device_id_type=MESH,
    )
    swap.start()
    swap.wait_recv()
    strips = [
        part[i] + part_in[:, starts[i]:starts[i + 1]].astype(F32) for i in range(SIDE)
    ]
    for i in range(SIDE):
        gram_ref[i * BLK:(i + 1) * BLK, i * BLK:] = strips[i].astype(BF16)
        for k in range(i + 1, SIDE):
            block = strips[i][:, (k - i) * BLK:(k - i + 1) * BLK]
            gram_ref[k * BLK:(k + 1) * BLK, i * BLK:(i + 1) * BLK] = block.T.astype(BF16)
    gram = gram_ref[...]
    square = jnp.dot(gram, gram, preferred_element_type=F32)
    gram32 = gram.astype(F32)
    poly = (B_COEF * gram32 + C_COEF * square).astype(BF16)
    poly32 = poly.astype(F32)

    turned = jnp.dot(poly, gram, preferred_element_type=F32)
    diagonal = lax.broadcasted_iota(jnp.int32, (KV_ROWS, KV_ROWS), 0) == lax.broadcasted_iota(
        jnp.int32, (KV_ROWS, KV_ROWS), 1
    )
    terms = (
        jnp.where(diagonal, (A_COEF * A_COEF) * gram32, 0.0)
        + (2 * A_COEF) * (poly32 * gram32)
        + turned * poly32
    )
    energy = jnp.sum(jnp.sum(terms, axis=0, keepdims=True), axis=1, keepdims=True)
    factor = lax.rsqrt(energy / (KV_ROWS * HALF) + eps)

    def to_new(q):
        return pltpu.make_async_remote_copy(
            src_ref=new_out.at[q], dst_ref=new_in.at[pl.ds(b * SIDE, SIDE)],
            send_sem=s4.at[q], recv_sem=r4.at[b], device_id=(group, device(a, q)), device_id_type=MESH,
        )

    def from_new(q):
        return pltpu.make_async_remote_copy(
            src_ref=new_out.at[q], dst_ref=new_in.at[pl.ds(q * SIDE, SIDE)],
            send_sem=s4.at[q], recv_sem=r4.at[q], device_id=(group, device(a, q)), device_id_type=MESH,
        )

    def update(q):
        block = mat[q]
        raw = A_COEF * block.astype(F32) + jnp.dot(poly, block, preferred_element_type=F32)
        return (raw * factor).astype(BF16).reshape(SIDE, BLK, SUB)

    for db in (2, 1, 3):
        q = shift(b, db)
        new_out[q] = update(q)
        to_new(q).start()
    new_in[pl.ds(b * SIDE, SIDE)] = update(b)
    for db in (1, 3, 2):
        from_new(shift(b, db)).wait_recv()

    def to_out(pa, pb):
        d = device(pa, pb)
        return pltpu.make_async_remote_copy(
            src_ref=out_blocks.at[d], dst_ref=out_ref.at[:, columns(a, b)],
            send_sem=s5.at[d], recv_sem=r5.at[me], device_id=(group, d), device_id_type=MESH,
        )

    def from_out(pa, pb):
        d = device(pa, pb)
        return pltpu.make_async_remote_copy(
            src_ref=out_blocks.at[d], dst_ref=out_ref.at[:, columns(pa, pb)],
            send_sem=s5.at[d], recv_sem=r5.at[d], device_id=(group, d), device_id_type=MESH,
        )

    for r in range(DEVS):
        out_blocks[r] = new_in[places[r]]
    for pa, pb in peers:
        to_out(pa, pb).start()
    own = pltpu.make_async_copy(out_blocks.at[me], out_ref.at[:, columns(a, b)], local_sem.at[1])
    own.start()
    own.wait()
    for pa, pb in peers:
        from_out(pa, pb).wait_recv()

    for pa, pb in peers:
        to_sub(pa, pb).wait_send()
        to_out(pa, pb).wait_send()
    for db in (1, 2, 3):
        to_mat(shift(b, db)).wait_send()
        to_new(shift(b, db)).wait_send()
    swap.wait_send()


def shards(iterate, block_matrix):
    dma = pltpu.SemaphoreType.DMA
    return pl.pallas_call(
        kernel,
        out_shape=jax.ShapeDtypeStruct(iterate.shape, BF16),
        in_specs=[pl.BlockSpec(memory_space=pl.ANY), pl.BlockSpec(memory_space=pl.ANY)],
        out_specs=pl.BlockSpec(memory_space=pl.ANY),
        scratch_shapes=[
            pltpu.SMEM((DEVS,), jnp.int32),
            pltpu.VMEM((DEVS, BLK, SUB), BF16),
            pltpu.VMEM((SIDE, KV_ROWS, SUB), BF16),
            pltpu.VMEM((SIDE, KV_ROWS, SUB), BF16),
            pltpu.VMEM((BLK, 10 * BLK), BF16),
            pltpu.VMEM((BLK, 10 * BLK), BF16),
            pltpu.VMEM((KV_ROWS, KV_ROWS), BF16),
            pltpu.VMEM((SIDE, SIDE, BLK, SUB), BF16),
            pltpu.VMEM((DEVS, BLK, SUB), BF16),
            pltpu.VMEM((DEVS, BLK, SUB), BF16),
            dma((3,)), pltpu.SemaphoreType.REGULAR,
            dma((DEVS,)), dma((DEVS,)),
            dma((SIDE,)), dma((SIDE,)),
            dma, dma,
            dma((SIDE,)), dma((SIDE,)),
            dma((DEVS,)), dma((DEVS,)),
        ],
        compiler_params=pltpu.CompilerParams(
            collective_id=0, has_side_effects=True, vmem_limit_bytes=63 * 1024 * 1024
        ),
        cost_estimate=pl.CostEstimate(flops=1_900_000_000, bytes_accessed=4_194_304, transcendentals=0),
    )(block_matrix, iterate)


def solution(mesh):
    return jax.shard_map(
        shards,
        mesh=mesh,
        in_specs=(P(("grp", "row"), None), P("grp")),
        out_specs=P(("grp", "row"), None),
        check_vma=False,
    )
```

```python
import jax
import jax.numpy as jnp
from jax import lax
from jax.experimental import pallas as pl
from jax.experimental.pallas import tpu as pltpu
from jax.sharding import PartitionSpec as P

BLK = 128
SIDE = 4
DEVS = SIDE * SIDE
SUB = 256
KV_ROWS = 512
HALF = 2048
STAGES = 2
WIDE = SUB // STAGES
MESH = pl.DeviceIdType.MESH

A_COEF = 3.4445
B_COEF = -4.775
C_COEF = 2.0315
eps = 1e-06
F32 = jnp.float32
BF16 = jnp.bfloat16


def kernel(
    owner_hbm, x_ref, out_ref,
    owner_ref, in_sub_0, in_sub_1, in_sorted, mat, part_out, part_in, gram_ref, new_out, new_in_0, new_in_1, out_blocks,
    local_sem, gate, s1, r1, s2, r2, s3, r3, s4, r4, s5, r5,
):
    in_sub = [in_sub_0, in_sub_1]
    new_in = [new_in_0, new_in_1]
    group = lax.axis_index("grp")
    me = lax.axis_index("row")
    turn = lax.rem(group, 2)
    y, x = me // SIDE, lax.rem(me, SIDE)
    a = y + turn * (x - y)
    b = x + turn * (y - x)
    step_a = SIDE - (SIDE - 1) * turn
    step_b = 1 + (SIDE - 1) * turn

    def device(a_, b_):
        return a_ * step_a + b_ * step_b

    def shift(v, d):
        return lax.rem(v + d, SIDE)

    a_peers = [(shift(a, d), b) for d in (2, 1, 3)]
    b_peers = [(a, shift(b, d)) for d in (2, 1, 3)]
    near = a_peers + b_peers
    far = [(shift(a, da), shift(b, db)) for da in (2, 1, 3) for db in (2, 1, 3)]
    peers = far + near

    def columns(a_, b_, s):
        return pl.ds(pl.multiple_of((a_ * SIDE + b_) * SUB + s * WIDE, WIDE), WIDE)

    def lanes(q):
        return pl.ds(pl.multiple_of(q * WIDE, WIDE), WIDE)

    def remote(src, dst, send, recv, peer):
        return pltpu.make_async_remote_copy(
            src_ref=src, dst_ref=dst, send_sem=send, recv_sem=recv,
            device_id=(group, peer), device_id_type=MESH,
        )

    fetch = pltpu.make_async_copy(owner_hbm, owner_ref, local_sem.at[0])
    fetch.start()
    barrier = pltpu.get_barrier_semaphore()
    for pa, pb in near:
        pl.semaphore_signal(barrier, inc=1, device_id=(group, device(pa, pb)), device_id_type=MESH)
    pl.semaphore_wait(barrier, len(near))
    for pa, pb in a_peers:
        pl.semaphore_signal(gate, inc=1, device_id=(group, device(pa, pb)), device_id_type=MESH)

    def to_sub(s, pa, pb):
        d = device(pa, pb)
        return remote(x_ref.at[:, columns(pa, pb, s)], in_sub[s].at[me], s1.at[s, d], r1.at[s, me], d)

    def from_sub(s, pa, pb):
        d = device(pa, pb)
        return remote(x_ref.at[:, columns(pa, pb, s)], in_sub[s].at[d], s1.at[s, d], r1.at[s, d], d)

    own = [
        pltpu.make_async_copy(x_ref.at[:, columns(a, b, s)], in_sub[s].at[me], local_sem.at[1 + s])
        for s in range(STAGES)
    ]
    for pa, pb in near:
        to_sub(0, pa, pb).start()
    pl.semaphore_wait(gate, SIDE - 1)
    for pa, pb in far:
        to_sub(0, pa, pb).start()
    for s in range(STAGES):
        own[s].start()
        if s:
            for pa, pb in peers:
                to_sub(s, pa, pb).start()

    fetch.wait()
    owners = [owner_ref[r] for r in range(DEVS)]
    places = []
    for r in range(DEVS):
        p = owners[r] * SIDE
        for q in range(r):
            p = p + jnp.where(owners[q] == owners[r], 1, 0)
        places.append(p)
    order = []
    for k in range(DEVS):
        o = jnp.int32(0)
        for r in range(1, DEVS):
            o = o + jnp.where(places[r] == k, r, 0)
        order.append(o)

    def to_mat(s, m):
        return remote(
            in_sorted.at[s, m], mat.at[s, :, lanes(b)], s2.at[s, m], r2.at[s, b], device(a, m)
        )

    def from_mat(s, q):
        return remote(
            in_sorted.at[s, q], mat.at[s, :, lanes(q)], s2.at[s, q], r2.at[s, q], device(a, q)
        )

    for s in range(STAGES):
        own[s].wait()
        for pa, pb in near + far:
            from_sub(s, pa, pb).wait_recv()
        for m in range(SIDE):
            for i in range(SIDE):
                in_sorted[s, m, i * BLK:(i + 1) * BLK, :] = in_sub[s][order[m * SIDE + i]]
        for _, pb in b_peers:
            to_mat(s, pb).start()
        mat[s, :, lanes(b)] = in_sorted[s, b]

    part = None
    for s in range(STAGES):
        for _, pb in b_peers:
            from_mat(s, pb).wait_recv()
        block = mat[s]
        new = lax.dot_general(block, block, (((1,), (1,)), ((), ())), preferred_element_type=F32)
        part = new if s == 0 else part + new
    starts = [0, 4 * BLK, 7 * BLK, 9 * BLK, 10 * BLK]
    for i in range(SIDE):
        part_out[:, starts[i]:starts[i + 1]] = part[i * BLK:(i + 1) * BLK, i * BLK:].astype(BF16)
    partner = a + 1 - 2 * lax.rem(a, 2)
    swap = remote(part_out, part_in, s3, r3, device(partner, b))
    swap.start()
    swap.wait_recv()
    for i in range(SIDE):
        strip = part[i * BLK:(i + 1) * BLK, i * BLK:] + part_in[:, starts[i]:starts[i + 1]].astype(F32)
        gram_ref[i * BLK:(i + 1) * BLK, i * BLK:] = strip.astype(BF16)
        for k in range(i + 1, SIDE):
            block = strip[:, (k - i) * BLK:(k - i + 1) * BLK]
            gram_ref[k * BLK:(k + 1) * BLK, i * BLK:(i + 1) * BLK] = block.T.astype(BF16)
    gram = gram_ref[...]
    square = jnp.dot(gram, gram, preferred_element_type=F32)
    gram32 = gram.astype(F32)
    poly = (B_COEF * gram32 + C_COEF * square).astype(BF16)
    poly32 = poly.astype(F32)

    turned = jnp.dot(poly, gram, preferred_element_type=F32)
    diagonal = lax.broadcasted_iota(jnp.int32, (KV_ROWS, KV_ROWS), 0) == lax.broadcasted_iota(
        jnp.int32, (KV_ROWS, KV_ROWS), 1
    )
    terms = (
        jnp.where(diagonal, (A_COEF * A_COEF) * gram32, 0.0)
        + (2 * A_COEF) * (poly32 * gram32)
        + turned * poly32
    )
    energy = jnp.sum(jnp.sum(terms, axis=0, keepdims=True), axis=1, keepdims=True)
    factor = lax.rsqrt(energy / (KV_ROWS * HALF) + eps)

    def to_new(s, q):
        return remote(
            new_out.at[s, q], new_in[s].at[pl.ds(b * SIDE, SIDE)], s4.at[s, q], r4.at[s, b], device(a, q)
        )

    def from_new(s, q):
        return remote(
            new_out.at[s, q], new_in[s].at[pl.ds(q * SIDE, SIDE)], s4.at[s, q], r4.at[s, q], device(a, q)
        )

    for s in range(STAGES):
        block = mat[s]
        raw = A_COEF * block.astype(F32) + jnp.dot(poly, block, preferred_element_type=F32)
        new = (raw * factor).astype(BF16)
        for q in range(SIDE):
            new_out[s, q] = new[:, q * WIDE:(q + 1) * WIDE].reshape(SIDE, BLK, WIDE)
        for _, pb in b_peers:
            to_new(s, pb).start()
        new_in[s][pl.ds(b * SIDE, SIDE)] = new_out[s, b]

    def to_out(s, pa, pb):
        d = device(pa, pb)
        return remote(out_blocks.at[s, d], out_ref.at[:, columns(a, b, s)], s5.at[s, d], r5.at[s, me], d)

    def from_out(s, pa, pb):
        d = device(pa, pb)
        return remote(out_blocks.at[s, d], out_ref.at[:, columns(pa, pb, s)], s5.at[s, d], r5.at[s, d], d)

    last = []
    for s in range(STAGES):
        for _, pb in b_peers:
            from_new(s, pb).wait_recv()
        for r in range(DEVS):
            out_blocks[s, r] = new_in[s][places[r]]
        for pa, pb in peers:
            to_out(s, pa, pb).start()
        own = pltpu.make_async_copy(
            out_blocks.at[s, me], out_ref.at[:, columns(a, b, s)], local_sem.at[1 + STAGES + s]
        )
        own.start()
        last.append(own)

    swap.wait_send()
    for s in range(STAGES):
        for pa, pb in peers:
            to_sub(s, pa, pb).wait_send()
        for _, pb in b_peers:
            to_mat(s, pb).wait_send()
            to_new(s, pb).wait_send()
    for s in range(STAGES):
        last[s].wait()
        for pa, pb in peers:
            from_out(s, pa, pb).wait_recv()
            to_out(s, pa, pb).wait_send()


def shards(iterate, block_matrix):
    dma = pltpu.SemaphoreType.DMA
    return pl.pallas_call(
        kernel,
        out_shape=pltpu.VMEM(iterate.shape, BF16),
        in_specs=[pl.BlockSpec(memory_space=pltpu.HBM), pl.BlockSpec(memory_space=pltpu.HBM)],
        out_specs=pl.BlockSpec(memory_space=pl.ANY),
        scratch_shapes=[
            pltpu.SMEM((DEVS,), jnp.int32),
            pltpu.VMEM((DEVS, BLK, WIDE), BF16),
            pltpu.VMEM((DEVS, BLK, WIDE), BF16),
            pltpu.VMEM((STAGES, SIDE, KV_ROWS, WIDE), BF16),
            pltpu.VMEM((STAGES, KV_ROWS, SIDE * WIDE), BF16),
            pltpu.VMEM((BLK, 10 * BLK), BF16),
            pltpu.VMEM((BLK, 10 * BLK), BF16),
            pltpu.VMEM((KV_ROWS, KV_ROWS), BF16),
            pltpu.VMEM((STAGES, SIDE, SIDE, BLK, WIDE), BF16),
            pltpu.VMEM((DEVS, BLK, WIDE), BF16),
            pltpu.VMEM((DEVS, BLK, WIDE), BF16),
            pltpu.VMEM((STAGES, DEVS, BLK, WIDE), BF16),
            dma((1 + 2 * STAGES,)), pltpu.SemaphoreType.REGULAR,
            dma((STAGES, DEVS)), dma((STAGES, DEVS)),
            dma((STAGES, SIDE)), dma((STAGES, SIDE)),
            dma, dma,
            dma((STAGES, SIDE)), dma((STAGES, SIDE)),
            dma((STAGES, DEVS)), dma((STAGES, DEVS)),
        ],
        compiler_params=pltpu.CompilerParams(
            collective_id=0, has_side_effects=True, vmem_limit_bytes=40 * 1024 * 1024
        ),
        cost_estimate=pl.CostEstimate(flops=1_900_000_000, bytes_accessed=4_194_304, transcendentals=0),
    )(
        pltpu.with_memory_space_constraint(block_matrix, pltpu.HBM),
        pltpu.with_memory_space_constraint(iterate, pltpu.HBM),
    )


def solution(mesh):
    return jax.shard_map(
        shards,
        mesh=mesh,
        in_specs=(P(("grp", "row"), None), P("grp")),
        out_specs=P(("grp", "row"), None),
        check_vma=False,
    )
```

```python
import jax
import jax.numpy as jnp
from jax import lax
from jax.experimental import pallas as pl
from jax.experimental.pallas import tpu as pltpu
from jax.sharding import PartitionSpec as P

BLK = 128
SIDE = 4
DEVS = SIDE * SIDE
SUB = 256
KV_ROWS = 512
HALF = 2048
STAGES = 2
WIDE = SUB // STAGES
MESH = pl.DeviceIdType.MESH

A_COEF = 3.4445
B_COEF = -4.775
C_COEF = 2.0315
eps = 1e-06
F32 = jnp.float32
BF16 = jnp.bfloat16


def kernel(
    owner_hbm, x_ref, out_ref,
    owner_ref, in_sub_0, in_sub_1, in_sorted, mat, part_out, part_in, gram_ref, new_out, new_in_0, new_in_1, out_blocks,
    local_sem, gate, s1, r1, s2, r2, s3, r3, s4, r4, s5, r5,
):
    in_sub = [in_sub_0, in_sub_1]
    new_in = [new_in_0, new_in_1]
    group = lax.axis_index("grp")
    me = lax.axis_index("row")
    turn = lax.rem(group, 2)
    y, x = me // SIDE, lax.rem(me, SIDE)
    a = y + turn * (x - y)
    b = x + turn * (y - x)
    step_a = SIDE - (SIDE - 1) * turn
    step_b = 1 + (SIDE - 1) * turn

    def device(a_, b_):
        return a_ * step_a + b_ * step_b

    def shift(v, d):
        return lax.rem(v + d, SIDE)

    a_peers = [(shift(a, d), b) for d in (2, 1, 3)]
    b_peers = [(a, shift(b, d)) for d in (2, 1, 3)]
    near = a_peers + b_peers
    far = [(shift(a, da), shift(b, db)) for da in (2, 1, 3) for db in (2, 1, 3)]
    peers = far + near

    def columns(a_, b_, s):
        return pl.ds(pl.multiple_of((a_ * SIDE + b_) * SUB + s * WIDE, WIDE), WIDE)

    def lanes(q):
        return pl.ds(pl.multiple_of(q * WIDE, WIDE), WIDE)

    def remote(src, dst, send, recv, peer):
        return pltpu.make_async_remote_copy(
            src_ref=src, dst_ref=dst, send_sem=send, recv_sem=recv,
            device_id=(group, peer), device_id_type=MESH,
        )

    fetch = pltpu.make_async_copy(owner_hbm, owner_ref, local_sem.at[0])
    fetch.start()
    barrier = pltpu.get_barrier_semaphore()
    for pa, pb in near:
        pl.semaphore_signal(barrier, inc=1, device_id=(group, device(pa, pb)), device_id_type=MESH)
    pl.semaphore_wait(barrier, len(near))
    for pa, pb in a_peers:
        pl.semaphore_signal(gate, inc=1, device_id=(group, device(pa, pb)), device_id_type=MESH)

    def to_sub(s, pa, pb):
        d = device(pa, pb)
        return remote(x_ref.at[:, columns(pa, pb, s)], in_sub[s].at[me], s1.at[s, d], r1.at[s, me], d)

    def from_sub(s, pa, pb):
        d = device(pa, pb)
        return remote(x_ref.at[:, columns(pa, pb, s)], in_sub[s].at[d], s1.at[s, d], r1.at[s, d], d)

    own = [
        pltpu.make_async_copy(x_ref.at[:, columns(a, b, s)], in_sub[s].at[me], local_sem.at[1 + s])
        for s in range(STAGES)
    ]
    for pa, pb in near:
        to_sub(0, pa, pb).start()
    pl.semaphore_wait(gate, SIDE - 1)
    for pa, pb in far:
        to_sub(0, pa, pb).start()
    for s in range(STAGES):
        own[s].start()
        if s:
            for pa, pb in peers:
                to_sub(s, pa, pb).start()

    fetch.wait()
    owners = [owner_ref[r] for r in range(DEVS)]
    places = []
    for r in range(DEVS):
        p = owners[r] * SIDE
        for q in range(r):
            p = p + jnp.where(owners[q] == owners[r], 1, 0)
        places.append(p)
    order = []
    for k in range(DEVS):
        o = jnp.int32(0)
        for r in range(1, DEVS):
            o = o + jnp.where(places[r] == k, r, 0)
        order.append(o)

    def to_mat(s, m):
        return remote(
            in_sorted.at[s, m], mat.at[s, :, lanes(b)], s2.at[s, m], r2.at[s, b], device(a, m)
        )

    def from_mat(s, q):
        return remote(
            in_sorted.at[s, q], mat.at[s, :, lanes(q)], s2.at[s, q], r2.at[s, q], device(a, q)
        )

    for s in range(STAGES):
        own[s].wait()
        for pa, pb in near + far:
            from_sub(s, pa, pb).wait_recv()
        for m in range(SIDE):
            for i in range(SIDE):
                in_sorted[s, m, i * BLK:(i + 1) * BLK, :] = in_sub[s][order[m * SIDE + i]]
        for _, pb in b_peers:
            to_mat(s, pb).start()
        mat[s, :, lanes(b)] = in_sorted[s, b]

    top = 2 * BLK
    for s in range(STAGES - 1):
        for _, pb in b_peers:
            from_mat(s, pb).wait_recv()
        block = mat[s]
        new = lax.dot_general(block, block, (((1,), (1,)), ((), ())), preferred_element_type=F32)
        part = new if s == 0 else part + new
    for _, pb in b_peers:
        from_mat(STAGES - 1, pb).wait_recv()
    block = mat[STAGES - 1]
    starts = [0, 4 * BLK, 7 * BLK, 9 * BLK, 10 * BLK]
    partner = a + 1 - 2 * lax.rem(a, 2)
    strips = []
    swaps = []
    for h in range(2):
        rows = slice(h * top, (h + 1) * top)
        new = lax.dot_general(
            block[rows], block[h * top:], (((1,), (1,)), ((), ())), preferred_element_type=F32
        ) + part[rows, h * top:]
        for k in range(2):
            i = 2 * h + k
            strips.append(new[k * BLK:(k + 1) * BLK, k * BLK:])
            part_out[:, starts[i]:starts[i + 1]] = strips[i].astype(BF16)
        piece = pl.ds(starts[2 * h], starts[2 * h + 2] - starts[2 * h])
        swap = remote(
            part_out.at[:, piece], part_in.at[:, piece], s3.at[h], r3.at[h], device(partner, b)
        )
        swap.start()
        swaps.append(swap)
    for i in range(SIDE):
        if i % 2 == 0:
            swaps[i // 2].wait_recv()
        strip = strips[i] + part_in[:, starts[i]:starts[i + 1]].astype(F32)
        gram_ref[i * BLK:(i + 1) * BLK, i * BLK:] = strip.astype(BF16)
        for k in range(i + 1, SIDE):
            block = strip[:, (k - i) * BLK:(k - i + 1) * BLK]
            gram_ref[k * BLK:(k + 1) * BLK, i * BLK:(i + 1) * BLK] = block.T.astype(BF16)
    gram = gram_ref[...]
    square = jnp.dot(gram, gram, preferred_element_type=F32)
    gram32 = gram.astype(F32)
    poly = (B_COEF * gram32 + C_COEF * square).astype(BF16)
    poly32 = poly.astype(F32)

    turned = jnp.dot(poly, gram, preferred_element_type=F32)
    diagonal = lax.broadcasted_iota(jnp.int32, (KV_ROWS, KV_ROWS), 0) == lax.broadcasted_iota(
        jnp.int32, (KV_ROWS, KV_ROWS), 1
    )
    terms = (
        jnp.where(diagonal, (A_COEF * A_COEF) * gram32, 0.0)
        + (2 * A_COEF) * (poly32 * gram32)
        + turned * poly32
    )
    energy = jnp.sum(jnp.sum(terms, axis=0, keepdims=True), axis=1, keepdims=True)
    factor = lax.rsqrt(energy / (KV_ROWS * HALF) + eps)

    def to_new(s, q):
        return remote(
            new_out.at[s, q], new_in[s].at[pl.ds(b * SIDE, SIDE)], s4.at[s, q], r4.at[s, b], device(a, q)
        )

    def from_new(s, q):
        return remote(
            new_out.at[s, q], new_in[s].at[pl.ds(q * SIDE, SIDE)], s4.at[s, q], r4.at[s, q], device(a, q)
        )

    for s in range(STAGES):
        block = mat[s]
        raw = A_COEF * block.astype(F32) + jnp.dot(poly, block, preferred_element_type=F32)
        new = (raw * factor).astype(BF16)
        for q in range(SIDE):
            new_out[s, q] = new[:, q * WIDE:(q + 1) * WIDE].reshape(SIDE, BLK, WIDE)
        for _, pb in b_peers:
            to_new(s, pb).start()
        new_in[s][pl.ds(b * SIDE, SIDE)] = new_out[s, b]

    def to_out(s, pa, pb):
        d = device(pa, pb)
        return remote(out_blocks.at[s, d], out_ref.at[:, columns(a, b, s)], s5.at[s, d], r5.at[s, me], d)

    def from_out(s, pa, pb):
        d = device(pa, pb)
        return remote(out_blocks.at[s, d], out_ref.at[:, columns(pa, pb, s)], s5.at[s, d], r5.at[s, d], d)

    last = []
    for s in range(STAGES):
        for _, pb in b_peers:
            from_new(s, pb).wait_recv()
        for r in range(DEVS):
            out_blocks[s, r] = new_in[s][places[r]]
        for pa, pb in peers:
            to_out(s, pa, pb).start()
        own = pltpu.make_async_copy(
            out_blocks.at[s, me], out_ref.at[:, columns(a, b, s)], local_sem.at[1 + STAGES + s]
        )
        own.start()
        last.append(own)

    for swap in swaps:
        swap.wait_send()
    for s in range(STAGES):
        for pa, pb in peers:
            to_sub(s, pa, pb).wait_send()
        for _, pb in b_peers:
            to_mat(s, pb).wait_send()
            to_new(s, pb).wait_send()
    for s in range(STAGES):
        last[s].wait()
        for pa, pb in peers:
            from_out(s, pa, pb).wait_recv()
            to_out(s, pa, pb).wait_send()


def shards(iterate, block_matrix):
    dma = pltpu.SemaphoreType.DMA
    return pl.pallas_call(
        kernel,
        out_shape=pltpu.VMEM(iterate.shape, BF16),
        in_specs=[pl.BlockSpec(memory_space=pltpu.HBM), pl.BlockSpec(memory_space=pltpu.HBM)],
        out_specs=pl.BlockSpec(memory_space=pl.ANY),
        scratch_shapes=[
            pltpu.SMEM((DEVS,), jnp.int32),
            pltpu.VMEM((DEVS, BLK, WIDE), BF16),
            pltpu.VMEM((DEVS, BLK, WIDE), BF16),
            pltpu.VMEM((STAGES, SIDE, KV_ROWS, WIDE), BF16),
            pltpu.VMEM((STAGES, KV_ROWS, SIDE * WIDE), BF16),
            pltpu.VMEM((BLK, 10 * BLK), BF16),
            pltpu.VMEM((BLK, 10 * BLK), BF16),
            pltpu.VMEM((KV_ROWS, KV_ROWS), BF16),
            pltpu.VMEM((STAGES, SIDE, SIDE, BLK, WIDE), BF16),
            pltpu.VMEM((DEVS, BLK, WIDE), BF16),
            pltpu.VMEM((DEVS, BLK, WIDE), BF16),
            pltpu.VMEM((STAGES, DEVS, BLK, WIDE), BF16),
            dma((1 + 2 * STAGES,)), pltpu.SemaphoreType.REGULAR,
            dma((STAGES, DEVS)), dma((STAGES, DEVS)),
            dma((STAGES, SIDE)), dma((STAGES, SIDE)),
            dma((2,)), dma((2,)),
            dma((STAGES, SIDE)), dma((STAGES, SIDE)),
            dma((STAGES, DEVS)), dma((STAGES, DEVS)),
        ],
        compiler_params=pltpu.CompilerParams(
            collective_id=0, has_side_effects=True, vmem_limit_bytes=40 * 1024 * 1024
        ),
        cost_estimate=pl.CostEstimate(flops=1_900_000_000, bytes_accessed=4_194_304, transcendentals=0),
    )(
        pltpu.with_memory_space_constraint(block_matrix, pltpu.HBM),
        pltpu.with_memory_space_constraint(iterate, pltpu.HBM),
    )


def solution(mesh):
    return jax.shard_map(
        shards,
        mesh=mesh,
        in_specs=(P(("grp", "row"), None), P("grp")),
        out_specs=P(("grp", "row"), None),
        check_vma=False,
    )
```

```python
import jax
import jax.numpy as jnp
from jax import lax
from jax.experimental import pallas as pl
from jax.experimental.pallas import tpu as pltpu
from jax.sharding import PartitionSpec as P

BLK = 128
SIDE = 4
DEVS = SIDE * SIDE
SUB = 256
KV_ROWS = 512
HALF = 2048
STAGES = 2
WIDE = SUB // STAGES
MESH = pl.DeviceIdType.MESH

A_COEF = 3.4445
B_COEF = -4.775
C_COEF = 2.0315
eps = 1e-06
F32 = jnp.float32
BF16 = jnp.bfloat16


def kernel(
    owner_hbm, x_ref, out_ref,
    owner_ref, in_sub_0, in_sub_1, in_sorted, mat, part_out, part_in, gram_ref, new_out, new_in_0, new_in_1, out_blocks,
    local_sem, gate, s1, r1, s2, r2, s3, r3, s4, r4, s5, r5,
):
    in_sub = [in_sub_0, in_sub_1]
    new_in = [new_in_0, new_in_1]
    group = lax.axis_index("grp")
    me = lax.axis_index("row")
    turn = lax.rem(group, 2)
    y, x = me // SIDE, lax.rem(me, SIDE)
    a = y + turn * (x - y)
    b = x + turn * (y - x)
    step_a = SIDE - (SIDE - 1) * turn
    step_b = 1 + (SIDE - 1) * turn

    def device(a_, b_):
        return a_ * step_a + b_ * step_b

    def shift(v, d):
        return lax.rem(v + d, SIDE)

    a_peers = [(shift(a, d), b) for d in (2, 1, 3)]
    b_peers = [(a, shift(b, d)) for d in (2, 1, 3)]
    near = a_peers + b_peers
    far = [(shift(a, da), shift(b, db)) for da in (2, 1, 3) for db in (2, 1, 3)]
    peers = far + near

    def columns(a_, b_, s):
        return pl.ds(pl.multiple_of((a_ * SIDE + b_) * SUB + s * WIDE, WIDE), WIDE)

    def lanes(q):
        return pl.ds(pl.multiple_of(q * WIDE, WIDE), WIDE)

    def remote(src, dst, send, recv, peer):
        return pltpu.make_async_remote_copy(
            src_ref=src, dst_ref=dst, send_sem=send, recv_sem=recv,
            device_id=(group, peer), device_id_type=MESH,
        )

    fetch = pltpu.make_async_copy(owner_hbm, owner_ref, local_sem.at[0])
    fetch.start()
    barrier = pltpu.get_barrier_semaphore()
    for pa, pb in near:
        pl.semaphore_signal(barrier, inc=1, device_id=(group, device(pa, pb)), device_id_type=MESH)
    pl.semaphore_wait(barrier, len(near))
    for pa, pb in a_peers:
        pl.semaphore_signal(gate, inc=1, device_id=(group, device(pa, pb)), device_id_type=MESH)

    def to_sub(s, pa, pb):
        d = device(pa, pb)
        return remote(x_ref.at[:, columns(pa, pb, s)], in_sub[s].at[me], s1.at[s], r1.at[s], d)

    def all_sub(s, n):
        blocks = in_sub[s].at[pl.ds(0, n)]
        return remote(blocks, blocks, s1.at[s], r1.at[s], device(*near[0]))

    own = [
        pltpu.make_async_copy(x_ref.at[:, columns(a, b, s)], in_sub[s].at[me], r1.at[s])
        for s in range(STAGES)
    ]
    for pa, pb in near:
        to_sub(0, pa, pb).start()
    pl.semaphore_wait(gate, SIDE - 1)
    for pa, pb in far:
        to_sub(0, pa, pb).start()
    for s in range(STAGES):
        own[s].start()
        if s:
            for pa, pb in peers:
                to_sub(s, pa, pb).start()

    fetch.wait()
    owners = [owner_ref[r] for r in range(DEVS)]
    places = []
    for r in range(DEVS):
        p = owners[r] * SIDE
        for q in range(r):
            p = p + jnp.where(owners[q] == owners[r], 1, 0)
        places.append(p)
    order = []
    for k in range(DEVS):
        o = jnp.int32(0)
        for r in range(1, DEVS):
            o = o + jnp.where(places[r] == k, r, 0)
        order.append(o)

    def to_mat(s, m):
        return remote(
            in_sorted.at[s, m], mat.at[s, :, lanes(b)], s2.at[s], r2.at[s], device(a, m)
        )

    def all_mat(s):
        blocks = in_sorted.at[s, pl.ds(0, SIDE - 1)]
        return remote(blocks, blocks, s2.at[s], r2.at[s], device(*near[0]))

    for s in range(STAGES):
        all_sub(s, DEVS).wait_recv()
        for m in range(SIDE):
            for i in range(SIDE):
                in_sorted[s, m, i * BLK:(i + 1) * BLK, :] = in_sub[s][order[m * SIDE + i]]
        for _, pb in b_peers:
            to_mat(s, pb).start()
        mat[s, :, lanes(b)] = in_sorted[s, b]

    top = 2 * BLK
    for s in range(STAGES - 1):
        all_mat(s).wait_recv()
        block = mat[s]
        new = lax.dot_general(block, block, (((1,), (1,)), ((), ())), preferred_element_type=F32)
        part = new if s == 0 else part + new
    all_mat(STAGES - 1).wait_recv()
    block = mat[STAGES - 1]
    starts = [0, 4 * BLK, 7 * BLK, 9 * BLK, 10 * BLK]
    partner = a + 1 - 2 * lax.rem(a, 2)
    strips = []
    swaps = []
    for h in range(2):
        rows = slice(h * top, (h + 1) * top)
        new = lax.dot_general(
            block[rows], block[h * top:], (((1,), (1,)), ((), ())), preferred_element_type=F32
        ) + part[rows, h * top:]
        for k in range(2):
            i = 2 * h + k
            strips.append(new[k * BLK:(k + 1) * BLK, k * BLK:])
            part_out[:, starts[i]:starts[i + 1]] = strips[i].astype(BF16)
        piece = pl.ds(starts[2 * h], starts[2 * h + 2] - starts[2 * h])
        swap = remote(
            part_out.at[:, piece], part_in.at[:, piece], s3.at[h], r3.at[h], device(partner, b)
        )
        swap.start()
        swaps.append(swap)
    for i in range(SIDE):
        if i % 2 == 0:
            swaps[i // 2].wait_recv()
        strip = strips[i] + part_in[:, starts[i]:starts[i + 1]].astype(F32)
        gram_ref[i * BLK:(i + 1) * BLK, i * BLK:] = strip.astype(BF16)
        for k in range(i + 1, SIDE):
            block = strip[:, (k - i) * BLK:(k - i + 1) * BLK]
            gram_ref[k * BLK:(k + 1) * BLK, i * BLK:(i + 1) * BLK] = block.T.astype(BF16)
    gram = gram_ref[...]
    square = jnp.dot(gram, gram, preferred_element_type=F32)
    gram32 = gram.astype(F32)
    poly = (B_COEF * gram32 + C_COEF * square).astype(BF16)
    poly32 = poly.astype(F32)

    turned = jnp.dot(poly, gram, preferred_element_type=F32)
    diagonal = lax.broadcasted_iota(jnp.int32, (KV_ROWS, KV_ROWS), 0) == lax.broadcasted_iota(
        jnp.int32, (KV_ROWS, KV_ROWS), 1
    )
    terms = (
        jnp.where(diagonal, (A_COEF * A_COEF) * gram32, 0.0)
        + (2 * A_COEF) * (poly32 * gram32)
        + turned * poly32
    )
    energy = jnp.sum(jnp.sum(terms, axis=0, keepdims=True), axis=1, keepdims=True)
    factor = lax.rsqrt(energy / (KV_ROWS * HALF) + eps)

    def to_new(s, q):
        return remote(
            new_out.at[s, q], new_in[s].at[pl.ds(b * SIDE, SIDE)], s4.at[s], r4.at[s], device(a, q)
        )

    def all_new(s):
        blocks = new_out.at[s, pl.ds(0, SIDE - 1)]
        return remote(blocks, blocks, s4.at[s], r4.at[s], device(*near[0]))

    for s in range(STAGES):
        block = mat[s]
        raw = A_COEF * block.astype(F32) + jnp.dot(poly, block, preferred_element_type=F32)
        new = (raw * factor).astype(BF16)
        for q in range(SIDE):
            new_out[s, q] = new[:, q * WIDE:(q + 1) * WIDE].reshape(SIDE, BLK, WIDE)
        for _, pb in b_peers:
            to_new(s, pb).start()
        new_in[s][pl.ds(b * SIDE, SIDE)] = new_out[s, b]

    def to_out(s, pa, pb):
        d = device(pa, pb)
        return remote(out_blocks.at[s, d], out_ref.at[:, columns(a, b, s)], s5.at[s], r5.at[s], d)

    def all_out(s, n):
        blocks = out_blocks.at[s, pl.ds(0, n)]
        return remote(blocks, blocks, s5.at[s], r5.at[s], device(*near[0]))

    for s in range(STAGES):
        all_new(s).wait_recv()
        for r in range(DEVS):
            out_blocks[s, r] = new_in[s][places[r]]
        for pa, pb in peers:
            to_out(s, pa, pb).start()
        pltpu.make_async_copy(out_blocks.at[s, me], out_ref.at[:, columns(a, b, s)], r5.at[s]).start()

    for swap in swaps:
        swap.wait_send()
    for s in range(STAGES):
        all_sub(s, DEVS - 1).wait_send()
        all_mat(s).wait_send()
        all_new(s).wait_send()
    for s in range(STAGES):
        all_out(s, DEVS).wait_recv()
        all_out(s, DEVS - 1).wait_send()


def shards(iterate, block_matrix):
    dma = pltpu.SemaphoreType.DMA
    return pl.pallas_call(
        kernel,
        out_shape=pltpu.VMEM(iterate.shape, BF16),
        in_specs=[pl.BlockSpec(memory_space=pltpu.HBM), pl.BlockSpec(memory_space=pltpu.HBM)],
        out_specs=pl.BlockSpec(memory_space=pl.ANY),
        scratch_shapes=[
            pltpu.SMEM((DEVS,), jnp.int32),
            pltpu.VMEM((DEVS, BLK, WIDE), BF16),
            pltpu.VMEM((DEVS, BLK, WIDE), BF16),
            pltpu.VMEM((STAGES, SIDE, KV_ROWS, WIDE), BF16),
            pltpu.VMEM((STAGES, KV_ROWS, SIDE * WIDE), BF16),
            pltpu.VMEM((BLK, 10 * BLK), BF16),
            pltpu.VMEM((BLK, 10 * BLK), BF16),
            pltpu.VMEM((KV_ROWS, KV_ROWS), BF16),
            pltpu.VMEM((STAGES, SIDE, SIDE, BLK, WIDE), BF16),
            pltpu.VMEM((DEVS, BLK, WIDE), BF16),
            pltpu.VMEM((DEVS, BLK, WIDE), BF16),
            pltpu.VMEM((STAGES, DEVS, BLK, WIDE), BF16),
            dma((1,)), pltpu.SemaphoreType.REGULAR,
            dma((STAGES,)), dma((STAGES,)),
            dma((STAGES,)), dma((STAGES,)),
            dma((2,)), dma((2,)),
            dma((STAGES,)), dma((STAGES,)),
            dma((STAGES,)), dma((STAGES,)),
        ],
        compiler_params=pltpu.CompilerParams(
            collective_id=0, has_side_effects=True, vmem_limit_bytes=40 * 1024 * 1024
        ),
        cost_estimate=pl.CostEstimate(flops=1_900_000_000, bytes_accessed=4_194_304, transcendentals=0),
    )(
        pltpu.with_memory_space_constraint(block_matrix, pltpu.HBM),
        pltpu.with_memory_space_constraint(iterate, pltpu.HBM),
    )


def solution(mesh):
    return jax.shard_map(
        shards,
        mesh=mesh,
        in_specs=(P(("grp", "row"), None), P("grp")),
        out_specs=P(("grp", "row"), None),
        check_vma=False,
    )
```

```python
import jax
import jax.numpy as jnp
from jax import lax
from jax.experimental import pallas as pl
from jax.experimental.pallas import tpu as pltpu
from jax.sharding import PartitionSpec as P

BLK = 128
SIDE = 4
DEVS = SIDE * SIDE
SUB = 256
KV_ROWS = 512
HALF = 2048
WIDE = 128
TALL = 64
TURNS = ((0, 0), (0, 1), (1, 0), (1, 1))
STAGES = len(TURNS)
TOP = SIDE * TALL
MESH = pl.DeviceIdType.MESH

A_COEF = 3.4445
B_COEF = -4.775
C_COEF = 2.0315
eps = 1e-06
F32 = jnp.float32
BF16 = jnp.bfloat16


def kernel(
    owner_hbm, x_ref, out_ref,
    owner_ref, in_sub_0, in_sub_1, in_sub_2, in_sub_3, in_sorted, mat, part_out, part_in, gram_ref, new_out,
    new_in_0, new_in_1, new_in_2, new_in_3, out_blocks,
    local_sem, gate, s1, r1, s2, r2, s3, r3, s4, r4, s5, r5,
):
    in_sub = [in_sub_0, in_sub_1, in_sub_2, in_sub_3]
    new_in = [new_in_0, new_in_1, new_in_2, new_in_3]
    group = lax.axis_index("grp")
    me = lax.axis_index("row")
    turn = lax.rem(group, 2)
    y, x = me // SIDE, lax.rem(me, SIDE)
    a = y + turn * (x - y)
    b = x + turn * (y - x)
    step_a = SIDE - (SIDE - 1) * turn
    step_b = 1 + (SIDE - 1) * turn

    def device(a_, b_):
        return a_ * step_a + b_ * step_b

    def shift(v, d):
        return lax.rem(v + d, SIDE)

    a_peers = [(shift(a, d), b) for d in (2, 1, 3)]
    b_peers = [(a, shift(b, d)) for d in (2, 1, 3)]
    near = a_peers + b_peers
    far = [(shift(a, da), shift(b, db)) for da in (2, 1, 3) for db in (2, 1, 3)]
    peers = far + near

    def piece(a_, b_, s):
        c, t = TURNS[s]
        return pl.ds(t * TALL, TALL), pl.ds(pl.multiple_of((a_ * SIDE + b_) * SUB + c * WIDE, WIDE), WIDE)

    def rows(s):
        return pl.ds(TURNS[s][1] * TOP, TOP)

    def lanes(q):
        return pl.ds(pl.multiple_of(q * WIDE, WIDE), WIDE)

    def remote(src, dst, send, recv, peer):
        return pltpu.make_async_remote_copy(
            src_ref=src, dst_ref=dst, send_sem=send, recv_sem=recv,
            device_id=(group, peer), device_id_type=MESH,
        )

    fetch = pltpu.make_async_copy(owner_hbm, owner_ref, local_sem.at[0])
    fetch.start()
    barrier = pltpu.get_barrier_semaphore()
    for pa, pb in near:
        pl.semaphore_signal(barrier, inc=1, device_id=(group, device(pa, pb)), device_id_type=MESH)
    pl.semaphore_wait(barrier, len(near))
    for pa, pb in a_peers:
        pl.semaphore_signal(gate, inc=1, device_id=(group, device(pa, pb)), device_id_type=MESH)

    def to_sub(s, pa, pb):
        d = device(pa, pb)
        return remote(x_ref.at[piece(pa, pb, s)], in_sub[s].at[me], s1.at[s], r1.at[s], d)

    def all_sub(s, n):
        blocks = in_sub[s].at[pl.ds(0, n)]
        return remote(blocks, blocks, s1.at[s], r1.at[s], device(*near[0]))

    own = [
        pltpu.make_async_copy(x_ref.at[piece(a, b, s)], in_sub[s].at[me], r1.at[s])
        for s in range(STAGES)
    ]
    for pa, pb in near:
        to_sub(0, pa, pb).start()
    pl.semaphore_wait(gate, SIDE - 1)
    for pa, pb in far:
        to_sub(0, pa, pb).start()
    for s in range(STAGES):
        own[s].start()
        if s:
            for pa, pb in peers:
                to_sub(s, pa, pb).start()

    fetch.wait()
    owners = [owner_ref[r] for r in range(DEVS)]
    places = []
    for r in range(DEVS):
        p = owners[r] * SIDE
        for q in range(r):
            p = p + jnp.where(owners[q] == owners[r], 1, 0)
        places.append(p)
    order = []
    for k in range(DEVS):
        o = jnp.int32(0)
        for r in range(1, DEVS):
            o = o + jnp.where(places[r] == k, r, 0)
        order.append(o)

    def to_mat(s, m):
        return remote(
            in_sorted.at[s, m], mat.at[TURNS[s][0], rows(s), lanes(b)], s2.at[s], r2.at[s], device(a, m)
        )

    def all_mat(s):
        blocks = in_sorted.at[s, pl.ds(0, SIDE - 1)]
        return remote(blocks, blocks, s2.at[s], r2.at[s], device(*near[0]))

    for s in range(STAGES):
        all_sub(s, DEVS).wait_recv()
        for m in range(SIDE):
            for i in range(SIDE):
                in_sorted[s, m, i * TALL:(i + 1) * TALL, :] = in_sub[s][order[m * SIDE + i]]
        for _, pb in b_peers:
            to_mat(s, pb).start()
        mat[TURNS[s][0], rows(s), lanes(b)] = in_sorted[s, b]

    def arrive(s):
        all_mat(s).wait_recv()

    def product(c, i, k):
        return lax.dot_general(
            mat[c, i * TOP:(i + 1) * TOP, :], mat[c, k * TOP:(k + 1) * TOP, :],
            (((1,), (1,)), ((), ())), preferred_element_type=F32,
        )

    partner = device(a + 1 - 2 * lax.rem(a, 2), b)

    def swap(n):
        span = pl.ds(0, 3 * BLK) if n == 0 else pl.ds(3 * BLK, 7 * BLK)
        return remote(part_out.at[:, span], part_in.at[:, span], s3.at[n], r3.at[n], partner)

    quads = ((0, 0), (0, 1), (1, 1))
    blocks = [
        [(0, 0), (0, 1), (1, 1)],
        [(0, 2), (0, 3), (1, 2), (1, 3), (2, 2), (2, 3), (3, 3)],
    ]
    arrive(0)
    arrive(1)
    part = {quad: product(0, *quad) for quad in quads}
    mine = {}
    for n in range(2):
        arrive(2 + n)
        for quad in quads[:1] if n == 0 else quads[1:]:
            part[quad] = part[quad] + product(1, *quad)
        for k, (i, j) in enumerate(blocks[n]):
            quad = part[i // 2, j // 2]
            mine[i, j] = quad[(i % 2) * BLK:(i % 2 + 1) * BLK, (j % 2) * BLK:(j % 2 + 1) * BLK]
            part_out[:, (3 * n + k) * BLK:(3 * n + k + 1) * BLK] = mine[i, j].astype(BF16)
        swap(n).start()
    for n in range(2):
        swap(n).wait_recv()
        for k, (i, j) in enumerate(blocks[n]):
            block = mine[i, j] + part_in[:, (3 * n + k) * BLK:(3 * n + k + 1) * BLK].astype(F32)
            gram_ref[i * BLK:(i + 1) * BLK, j * BLK:(j + 1) * BLK] = block.astype(BF16)
            if i != j:
                gram_ref[j * BLK:(j + 1) * BLK, i * BLK:(i + 1) * BLK] = block.T.astype(BF16)
    gram = gram_ref[...]
    square = jnp.dot(gram, gram, preferred_element_type=F32)
    gram32 = gram.astype(F32)
    poly = (B_COEF * gram32 + C_COEF * square).astype(BF16)
    poly32 = poly.astype(F32)

    turned = jnp.dot(poly, gram, preferred_element_type=F32)
    diagonal = lax.broadcasted_iota(jnp.int32, (KV_ROWS, KV_ROWS), 0) == lax.broadcasted_iota(
        jnp.int32, (KV_ROWS, KV_ROWS), 1
    )
    terms = (
        jnp.where(diagonal, (A_COEF * A_COEF) * gram32, 0.0)
        + (2 * A_COEF) * (poly32 * gram32)
        + turned * poly32
    )
    energy = jnp.sum(jnp.sum(terms, axis=0, keepdims=True), axis=1, keepdims=True)
    factor = lax.rsqrt(energy / (KV_ROWS * HALF) + eps)

    def to_new(s, q):
        return remote(
            new_out.at[s, q], new_in[s].at[pl.ds(b * SIDE, SIDE)], s4.at[s], r4.at[s], device(a, q)
        )

    def all_new(s):
        blocks = new_out.at[s, pl.ds(0, SIDE - 1)]
        return remote(blocks, blocks, s4.at[s], r4.at[s], device(*near[0]))

    for s in range(STAGES):
        c, t = TURNS[s]
        raw = A_COEF * mat[c, t * TOP:(t + 1) * TOP, :].astype(F32) + jnp.dot(
            poly[t * TOP:(t + 1) * TOP, :], mat[c], preferred_element_type=F32
        )
        new = (raw * factor).astype(BF16)
        for q in range(SIDE):
            new_out[s, q] = new[:, q * WIDE:(q + 1) * WIDE].reshape(SIDE, TALL, WIDE)
        for _, pb in b_peers:
            to_new(s, pb).start()
        new_in[s][pl.ds(b * SIDE, SIDE)] = new_out[s, b]

    def to_out(s, pa, pb):
        d = device(pa, pb)
        return remote(out_blocks.at[s, d], out_ref.at[piece(a, b, s)], s5.at[s], r5.at[s], d)

    def all_out(s, n):
        blocks = out_blocks.at[s, pl.ds(0, n)]
        return remote(blocks, blocks, s5.at[s], r5.at[s], device(*near[0]))

    for s in range(STAGES):
        all_new(s).wait_recv()
        for r in range(DEVS):
            out_blocks[s, r] = new_in[s][places[r]]
        for pa, pb in peers:
            to_out(s, pa, pb).start()
        pltpu.make_async_copy(out_blocks.at[s, me], out_ref.at[piece(a, b, s)], r5.at[s]).start()

    for n in range(2):
        swap(n).wait_send()
    for s in range(STAGES):
        all_sub(s, DEVS - 1).wait_send()
        all_mat(s).wait_send()
        all_new(s).wait_send()
    for s in range(STAGES):
        all_out(s, DEVS).wait_recv()
        all_out(s, DEVS - 1).wait_send()


def shards(iterate, block_matrix):
    dma = pltpu.SemaphoreType.DMA
    return pl.pallas_call(
        kernel,
        out_shape=pltpu.VMEM(iterate.shape, BF16),
        in_specs=[pl.BlockSpec(memory_space=pltpu.HBM), pl.BlockSpec(memory_space=pltpu.HBM)],
        out_specs=pl.BlockSpec(memory_space=pl.ANY),
        scratch_shapes=[
            pltpu.SMEM((DEVS,), jnp.int32),
            *[pltpu.VMEM((DEVS, TALL, WIDE), BF16)] * STAGES,
            pltpu.VMEM((STAGES, SIDE, TOP, WIDE), BF16),
            pltpu.VMEM((2, KV_ROWS, SIDE * WIDE), BF16),
            pltpu.VMEM((BLK, 10 * BLK), BF16),
            pltpu.VMEM((BLK, 10 * BLK), BF16),
            pltpu.VMEM((KV_ROWS, KV_ROWS), BF16),
            pltpu.VMEM((STAGES, SIDE, SIDE, TALL, WIDE), BF16),
            *[pltpu.VMEM((DEVS, TALL, WIDE), BF16)] * STAGES,
            pltpu.VMEM((STAGES, DEVS, TALL, WIDE), BF16),
            dma((1,)), pltpu.SemaphoreType.REGULAR,
            dma((STAGES,)), dma((STAGES,)),
            dma((STAGES,)), dma((STAGES,)),
            dma((2,)), dma((2,)),
            dma((STAGES,)), dma((STAGES,)),
            dma((STAGES,)), dma((STAGES,)),
        ],
        compiler_params=pltpu.CompilerParams(
            collective_id=0, has_side_effects=True, vmem_limit_bytes=40 * 1024 * 1024
        ),
        cost_estimate=pl.CostEstimate(flops=1_900_000_000, bytes_accessed=4_194_304, transcendentals=0),
    )(
        pltpu.with_memory_space_constraint(block_matrix, pltpu.HBM),
        pltpu.with_memory_space_constraint(iterate, pltpu.HBM),
    )


def solution(mesh):
    return jax.shard_map(
        shards,
        mesh=mesh,
        in_specs=(P(("grp", "row"), None), P("grp")),
        out_specs=P(("grp", "row"), None),
        check_vma=False,
    )
```

```python
import jax
import jax.numpy as jnp
from jax import lax
from jax.experimental import pallas as pl
from jax.experimental.pallas import tpu as pltpu
from jax.sharding import PartitionSpec as P

BLK = 128
SIDE = 4
DEVS = SIDE * SIDE
SUB = 256
KV_ROWS = 512
HALF = 2048
WIDE = 128
TALLS = (64, 64)
TURNS = ((0, (0, 1)), (1, (0,)), (1, (1,)))
WAY_BACK = (1, 2, 0)
STAGES = len(TURNS)
TOP = SIDE * TALLS[0]
MESH = pl.DeviceIdType.MESH

A_COEF = 3.4445
B_COEF = -4.775
C_COEF = 2.0315
eps = 1e-06
F32 = jnp.float32
BF16 = jnp.bfloat16


def height(ts):
    return sum(TALLS[t] for t in ts)


def kernel(
    owner_hbm, x_ref, out_ref,
    owner_ref, mat, part_out, part_in, gram_ref, *refs,
):
    in_sub, in_sorted, new_out, new_in, out_blocks = (refs[i * STAGES:(i + 1) * STAGES] for i in range(5))
    local_sem, gate, s1, r1, s2, r2, s3, r3, s4, r4, s5, r5 = refs[5 * STAGES:]
    group = lax.axis_index("grp")
    me = lax.axis_index("row")
    turn = lax.rem(group, 2)
    y, x = me // SIDE, lax.rem(me, SIDE)
    a = y + turn * (x - y)
    b = x + turn * (y - x)
    step_a = SIDE - (SIDE - 1) * turn
    step_b = 1 + (SIDE - 1) * turn

    def device(a_, b_):
        return a_ * step_a + b_ * step_b

    def shift(v, d):
        return lax.rem(v + d, SIDE)

    a_peers = [(shift(a, d), b) for d in (2, 1, 3)]
    b_peers = [(a, shift(b, d)) for d in (2, 1, 3)]
    near = a_peers + b_peers
    far = [(shift(a, da), shift(b, db)) for da in (2, 1, 3) for db in (2, 1, 3)]
    peers = far + near

    def piece(a_, b_, s):
        c, ts = TURNS[s]
        return pl.ds(ts[0] * TALLS[0], height(ts)), pl.ds(pl.multiple_of((a_ * SIDE + b_) * SUB + c * WIDE, WIDE), WIDE)

    def rows(s):
        ts = TURNS[s][1]
        return pl.ds(ts[0] * TOP, SIDE * height(ts))

    def lanes(q):
        return pl.ds(pl.multiple_of(q * WIDE, WIDE), WIDE)

    def remote(src, dst, send, recv, peer):
        return pltpu.make_async_remote_copy(
            src_ref=src, dst_ref=dst, send_sem=send, recv_sem=recv,
            device_id=(group, peer), device_id_type=MESH,
        )

    fetch = pltpu.make_async_copy(owner_hbm, owner_ref, local_sem.at[0])
    fetch.start()
    barrier = pltpu.get_barrier_semaphore()
    for pa, pb in near:
        pl.semaphore_signal(barrier, inc=1, device_id=(group, device(pa, pb)), device_id_type=MESH)
    pl.semaphore_wait(barrier, len(near))
    for pa, pb in a_peers:
        pl.semaphore_signal(gate, inc=1, device_id=(group, device(pa, pb)), device_id_type=MESH)

    def to_sub(s, pa, pb):
        d = device(pa, pb)
        return remote(x_ref.at[piece(pa, pb, s)], in_sub[s].at[me], s1.at[s], r1.at[s], d)

    def all_sub(s, n):
        blocks = in_sub[s].at[pl.ds(0, n)]
        return remote(blocks, blocks, s1.at[s], r1.at[s], device(*near[0]))

    own = [
        pltpu.make_async_copy(x_ref.at[piece(a, b, s)], in_sub[s].at[me], r1.at[s])
        for s in range(STAGES)
    ]
    for pa, pb in near:
        to_sub(0, pa, pb).start()
    pl.semaphore_wait(gate, SIDE - 1)
    for pa, pb in far:
        to_sub(0, pa, pb).start()
    for s in range(STAGES):
        own[s].start()
        if s:
            for pa, pb in peers:
                to_sub(s, pa, pb).start()

    fetch.wait()
    owners = [owner_ref[r] for r in range(DEVS)]
    places = []
    for r in range(DEVS):
        p = owners[r] * SIDE
        for q in range(r):
            p = p + jnp.where(owners[q] == owners[r], 1, 0)
        places.append(p)
    order = []
    for k in range(DEVS):
        o = jnp.int32(0)
        for r in range(1, DEVS):
            o = o + jnp.where(places[r] == k, r, 0)
        order.append(o)

    def to_mat(s, m):
        return remote(
            in_sorted[s].at[m], mat.at[TURNS[s][0], rows(s), lanes(b)], s2.at[s], r2.at[s], device(a, m)
        )

    def all_mat(s):
        blocks = in_sorted[s].at[pl.ds(0, SIDE - 1)]
        return remote(blocks, blocks, s2.at[s], r2.at[s], device(*near[0]))

    for s in range(STAGES):
        all_sub(s, DEVS).wait_recv()
        for m in range(SIDE):
            for i in range(SIDE):
                block = in_sub[s][order[m * SIDE + i]]
                for n, t in enumerate(TURNS[s][1]):
                    tall = TALLS[t]
                    first = n * TOP + i * tall
                    in_sorted[s][m, first:first + tall, :] = block[n * TALLS[0]:n * TALLS[0] + tall]
        for _, pb in b_peers:
            to_mat(s, pb).start()
        mat[TURNS[s][0], rows(s), lanes(b)] = in_sorted[s][b]

    def arrive(s):
        all_mat(s).wait_recv()

    ends = ((0, TOP), (TOP, KV_ROWS))

    def product(c, i, k):
        return lax.dot_general(
            mat[c, ends[i][0]:ends[i][1], :], mat[c, ends[k][0]:ends[k][1], :],
            (((1,), (1,)), ((), ())), preferred_element_type=F32,
        )

    partner = device(a + 1 - 2 * lax.rem(a, 2), b)

    quads = ((0, 0), (0, 1), (1, 1))
    edge = TOP // BLK
    pairs = [(i, j) for i in range(SIDE) for j in range(i, SIDE)]
    blocks = [[p for p in pairs if p[1] < edge], [p for p in pairs if p[1] >= edge]]
    starts = [0, len(blocks[0])]

    def swap(n):
        span = pl.ds(starts[n] * BLK, len(blocks[n]) * BLK)
        return remote(part_out.at[:, span], part_in.at[:, span], s3.at[n], r3.at[n], partner)

    arrive(0)
    part = {quad: product(0, *quad) for quad in quads}
    mine = {}
    for n in range(2):
        arrive(1 + n)
        for quad in quads[:1] if n == 0 else quads[1:]:
            part[quad] = part[quad] + product(1, *quad)
        for k, (i, j) in enumerate(blocks[n]):
            quad = part[i // edge, j // edge]
            u, v = i % edge * BLK, j % edge * BLK
            mine[i, j] = quad[u:u + BLK, v:v + BLK]
            part_out[:, (starts[n] + k) * BLK:(starts[n] + k + 1) * BLK] = mine[i, j].astype(BF16)
        swap(n).start()
    for n in range(2):
        swap(n).wait_recv()
        for k, (i, j) in enumerate(blocks[n]):
            block = mine[i, j] + part_in[:, (starts[n] + k) * BLK:(starts[n] + k + 1) * BLK].astype(F32)
            gram_ref[i * BLK:(i + 1) * BLK, j * BLK:(j + 1) * BLK] = block.astype(BF16)
            if i != j:
                gram_ref[j * BLK:(j + 1) * BLK, i * BLK:(i + 1) * BLK] = block.T.astype(BF16)
    gram = gram_ref[...]
    square = jnp.dot(gram, gram, preferred_element_type=F32)
    gram32 = gram.astype(F32)
    poly = (B_COEF * gram32 + C_COEF * square).astype(BF16)
    poly32 = poly.astype(F32)

    turned = jnp.dot(poly, gram, preferred_element_type=F32)
    diagonal = lax.broadcasted_iota(jnp.int32, (KV_ROWS, KV_ROWS), 0) == lax.broadcasted_iota(
        jnp.int32, (KV_ROWS, KV_ROWS), 1
    )
    terms = (
        jnp.where(diagonal, (A_COEF * A_COEF) * gram32, 0.0)
        + (2 * A_COEF) * (poly32 * gram32)
        + turned * poly32
    )
    energy = jnp.sum(jnp.sum(terms, axis=0, keepdims=True), axis=1, keepdims=True)
    factor = lax.rsqrt(energy / (KV_ROWS * HALF) + eps)

    def to_new(s, q):
        return remote(
            new_out[s].at[q], new_in[s].at[pl.ds(b * SIDE, SIDE)], s4.at[s], r4.at[s], device(a, q)
        )

    def all_new(s):
        blocks = new_out[s].at[pl.ds(0, SIDE - 1)]
        return remote(blocks, blocks, s4.at[s], r4.at[s], device(*near[0]))

    for s in WAY_BACK:
        c, ts = TURNS[s]
        first, last = ends[ts[0]][0], ends[ts[-1]][1]
        raw = A_COEF * mat[c, first:last, :].astype(F32) + jnp.dot(
            poly[first:last, :], mat[c], preferred_element_type=F32
        )
        new = (raw * factor).astype(BF16)
        for q in range(SIDE):
            for n, t in enumerate(ts):
                rows_t = new[n * TOP:n * TOP + SIDE * TALLS[t], q * WIDE:(q + 1) * WIDE]
                new_out[s][q, :, n * TALLS[0]:n * TALLS[0] + TALLS[t], :] = rows_t.reshape(SIDE, TALLS[t], WIDE)
        for _, pb in b_peers:
            to_new(s, pb).start()
        new_in[s][pl.ds(b * SIDE, SIDE)] = new_out[s][b]

    def to_out(s, pa, pb):
        d = device(pa, pb)
        return remote(out_blocks[s].at[d], out_ref.at[piece(a, b, s)], s5.at[s], r5.at[s], d)

    def all_out(s, n):
        blocks = out_blocks[s].at[pl.ds(0, n)]
        return remote(blocks, blocks, s5.at[s], r5.at[s], device(*near[0]))

    for s in WAY_BACK:
        all_new(s).wait_recv()
        for r in range(DEVS):
            out_blocks[s][r] = new_in[s][places[r]]
        for pa, pb in peers:
            to_out(s, pa, pb).start()
        pltpu.make_async_copy(out_blocks[s].at[me], out_ref.at[piece(a, b, s)], r5.at[s]).start()

    for n in range(2):
        swap(n).wait_send()
    for s in range(STAGES):
        all_sub(s, DEVS - 1).wait_send()
        all_mat(s).wait_send()
        all_new(s).wait_send()
    for s in range(STAGES):
        all_out(s, DEVS).wait_recv()
        all_out(s, DEVS - 1).wait_send()


def shards(iterate, block_matrix):
    dma = pltpu.SemaphoreType.DMA

    def buffers(lead):
        return [pltpu.VMEM((*lead(height(ts)), WIDE), BF16) for _, ts in TURNS]

    return pl.pallas_call(
        kernel,
        out_shape=pltpu.VMEM(iterate.shape, BF16),
        in_specs=[pl.BlockSpec(memory_space=pltpu.HBM), pl.BlockSpec(memory_space=pltpu.HBM)],
        out_specs=pl.BlockSpec(memory_space=pl.ANY),
        scratch_shapes=[
            pltpu.SMEM((DEVS,), jnp.int32),
            pltpu.VMEM((2, KV_ROWS, SIDE * WIDE), BF16),
            pltpu.VMEM((BLK, 10 * BLK), BF16),
            pltpu.VMEM((BLK, 10 * BLK), BF16),
            pltpu.VMEM((KV_ROWS, KV_ROWS), BF16),
            *buffers(lambda tall: (DEVS, tall)),
            *buffers(lambda tall: (SIDE, SIDE * tall)),
            *buffers(lambda tall: (SIDE, SIDE, tall)),
            *buffers(lambda tall: (DEVS, tall)),
            *buffers(lambda tall: (DEVS, tall)),
            dma((1,)), pltpu.SemaphoreType.REGULAR,
            dma((STAGES,)), dma((STAGES,)),
            dma((STAGES,)), dma((STAGES,)),
            dma((2,)), dma((2,)),
            dma((STAGES,)), dma((STAGES,)),
            dma((STAGES,)), dma((STAGES,)),
        ],
        compiler_params=pltpu.CompilerParams(
            collective_id=0, has_side_effects=True, vmem_limit_bytes=40 * 1024 * 1024
        ),
        cost_estimate=pl.CostEstimate(flops=1_900_000_000, bytes_accessed=4_194_304, transcendentals=0),
    )(
        pltpu.with_memory_space_constraint(block_matrix, pltpu.HBM),
        pltpu.with_memory_space_constraint(iterate, pltpu.HBM),
    )


def solution(mesh):
    return jax.shard_map(
        shards,
        mesh=mesh,
        in_specs=(P(("grp", "row"), None), P("grp")),
        out_specs=P(("grp", "row"), None),
        check_vma=False,
    )
```

```python
import jax
import jax.numpy as jnp
from jax import lax
from jax.experimental import pallas as pl
from jax.experimental.pallas import tpu as pltpu
from jax.sharding import PartitionSpec as P

BLK = 128
SIDE = 4
DEVS = SIDE * SIDE
SUB = 256
KV_ROWS = 512
HALF = 2048
WIDE = 128
TALLS = (64, 64)
TURNS = ((0, (0, 1)), (1, (0,)), (1, (1,)))
WAY_BACK = (1, 2, 0)
STAGES = len(TURNS)
TOP = SIDE * TALLS[0]
MESH = pl.DeviceIdType.MESH

A_COEF = 3.4445
B_COEF = -4.775
C_COEF = 2.0315
eps = 1e-06
F32 = jnp.float32
BF16 = jnp.bfloat16


def height(ts):
    return sum(TALLS[t] for t in ts)


def kernel(
    owner_hbm, x_ref, out_ref,
    owner_ref, mat, part_out, part_in, gram_ref, *refs,
):
    in_sub, in_sorted, new_out, new_in, out_blocks = (refs[i * STAGES:(i + 1) * STAGES] for i in range(5))
    local_sem, gate, s1, r1, s2, r2, s3, r3, s4, r4, s5, r5 = refs[5 * STAGES:]
    group = lax.axis_index("grp")
    me = lax.axis_index("row")
    turn = lax.rem(group, 2)
    y, x = me // SIDE, lax.rem(me, SIDE)
    a = y + turn * (x - y)
    b = x + turn * (y - x)
    step_a = SIDE - (SIDE - 1) * turn
    step_b = 1 + (SIDE - 1) * turn

    def device(a_, b_):
        return a_ * step_a + b_ * step_b

    def shift(v, d):
        return lax.rem(v + d, SIDE)

    a_peers = [(shift(a, d), b) for d in (2, 1, 3)]
    b_peers = [(a, shift(b, d)) for d in (2, 1, 3)]
    near = a_peers + b_peers
    far = [(shift(a, da), shift(b, db)) for da in (2, 1, 3) for db in (2, 1, 3)]
    peers = far + near

    def piece(a_, b_, s):
        c, ts = TURNS[s]
        return pl.ds(ts[0] * TALLS[0], height(ts)), pl.ds(pl.multiple_of((a_ * SIDE + b_) * SUB + c * WIDE, WIDE), WIDE)

    def rows(s):
        ts = TURNS[s][1]
        return pl.ds(ts[0] * TOP, SIDE * height(ts))

    def lanes(q):
        return pl.ds(pl.multiple_of(q * WIDE, WIDE), WIDE)

    def remote(src, dst, send, recv, peer):
        return pltpu.make_async_remote_copy(
            src_ref=src, dst_ref=dst, send_sem=send, recv_sem=recv,
            device_id=(group, peer), device_id_type=MESH,
        )

    fetch = pltpu.make_async_copy(owner_hbm, owner_ref, local_sem.at[0])
    fetch.start()
    barrier = pltpu.get_barrier_semaphore()
    for pa, pb in near:
        pl.semaphore_signal(barrier, inc=1, device_id=(group, device(pa, pb)), device_id_type=MESH)
    pl.semaphore_wait(barrier, len(near))
    for pa, pb in a_peers:
        pl.semaphore_signal(gate, inc=1, device_id=(group, device(pa, pb)), device_id_type=MESH)

    def to_sub(s, pa, pb):
        d = device(pa, pb)
        return remote(x_ref.at[piece(pa, pb, s)], in_sub[s].at[me], s1.at[s], r1.at[s], d)

    def all_sub(s, n):
        blocks = in_sub[s].at[pl.ds(0, n)]
        return remote(blocks, blocks, s1.at[s], r1.at[s], device(*near[0]))

    own = [
        pltpu.make_async_copy(x_ref.at[piece(a, b, s)], in_sub[s].at[me], r1.at[s])
        for s in range(STAGES)
    ]
    for s in range(2):
        for pa, pb in near:
            to_sub(s, pa, pb).start()
    pl.semaphore_wait(gate, SIDE - 1)
    for s in range(STAGES):
        for pa, pb in far if s < 2 else peers:
            to_sub(s, pa, pb).start()
        own[s].start()

    fetch.wait()
    owners = [owner_ref[r] for r in range(DEVS)]
    places = []
    for r in range(DEVS):
        p = owners[r] * SIDE
        for q in range(r):
            p = p + jnp.where(owners[q] == owners[r], 1, 0)
        places.append(p)
    order = []
    for k in range(DEVS):
        o = jnp.int32(0)
        for r in range(1, DEVS):
            o = o + jnp.where(places[r] == k, r, 0)
        order.append(o)

    order_at = [
        [sum(jnp.where(shift(b, d) == m, order[m * SIDE + i], 0) for m in range(SIDE)) for i in range(SIDE)]
        for d in range(SIDE)
    ]
    place_at = [
        sum(jnp.where(device(pa, pb) == r, places[r], 0) for r in range(DEVS)) for pa, pb in peers + [(a, b)]
    ]

    def to_mat(s, d):
        return remote(
            in_sorted[s].at[d], mat.at[TURNS[s][0], rows(s), lanes(b)], s2.at[s], r2.at[s],
            device(a, shift(b, d)),
        )

    def all_mat(s):
        blocks = in_sorted[s].at[pl.ds(0, SIDE - 1)]
        return remote(blocks, blocks, s2.at[s], r2.at[s], device(*near[0]))

    for s in range(STAGES):
        all_sub(s, DEVS).wait_recv()
        for d in (2, 1, 3, 0):
            for i in range(SIDE):
                block = in_sub[s][order_at[d][i]]
                for n, t in enumerate(TURNS[s][1]):
                    tall = TALLS[t]
                    first = n * TOP + i * tall
                    in_sorted[s][d, first:first + tall, :] = block[n * TALLS[0]:n * TALLS[0] + tall]
            if d:
                to_mat(s, d).start()
        mat[TURNS[s][0], rows(s), lanes(b)] = in_sorted[s][0]

    def arrive(s):
        all_mat(s).wait_recv()

    ends = ((0, TOP), (TOP, KV_ROWS))

    def product(c, i, k):
        return lax.dot_general(
            mat[c, ends[i][0]:ends[i][1], :], mat[c, ends[k][0]:ends[k][1], :],
            (((1,), (1,)), ((), ())), preferred_element_type=F32,
        )

    partner = device(a + 1 - 2 * lax.rem(a, 2), b)

    quads = ((0, 0), (0, 1), (1, 1))
    edge = TOP // BLK
    pairs = [(i, j) for i in range(SIDE) for j in range(i, SIDE)]
    blocks = [[p for p in pairs if p[1] < edge], [p for p in pairs if p[1] >= edge]]
    starts = [0, len(blocks[0])]

    def swap(n):
        span = pl.ds(starts[n] * BLK, len(blocks[n]) * BLK)
        return remote(part_out.at[:, span], part_in.at[:, span], s3.at[n], r3.at[n], partner)

    arrive(0)
    part = {quad: product(0, *quad) for quad in quads}
    mine = {}
    for n in range(2):
        arrive(1 + n)
        for quad in quads[:1] if n == 0 else quads[1:]:
            part[quad] = part[quad] + product(1, *quad)
        for k, (i, j) in enumerate(blocks[n]):
            quad = part[i // edge, j // edge]
            u, v = i % edge * BLK, j % edge * BLK
            mine[i, j] = quad[u:u + BLK, v:v + BLK]
            part_out[:, (starts[n] + k) * BLK:(starts[n] + k + 1) * BLK] = mine[i, j].astype(BF16)
        swap(n).start()
    for n in range(2):
        swap(n).wait_recv()
        for k, (i, j) in enumerate(blocks[n]):
            block = mine[i, j] + part_in[:, (starts[n] + k) * BLK:(starts[n] + k + 1) * BLK].astype(F32)
            gram_ref[i * BLK:(i + 1) * BLK, j * BLK:(j + 1) * BLK] = block.astype(BF16)
            if i != j:
                gram_ref[j * BLK:(j + 1) * BLK, i * BLK:(i + 1) * BLK] = block.T.astype(BF16)
    gram = gram_ref[...]
    square = jnp.dot(gram, gram, preferred_element_type=F32)
    gram32 = gram.astype(F32)
    poly = (B_COEF * gram32 + C_COEF * square).astype(BF16)
    poly32 = poly.astype(F32)

    turned = jnp.dot(poly, gram, preferred_element_type=F32)
    diagonal = lax.broadcasted_iota(jnp.int32, (KV_ROWS, KV_ROWS), 0) == lax.broadcasted_iota(
        jnp.int32, (KV_ROWS, KV_ROWS), 1
    )
    terms = (
        jnp.where(diagonal, (A_COEF * A_COEF) * gram32, 0.0)
        + (2 * A_COEF) * (poly32 * gram32)
        + turned * poly32
    )
    energy = jnp.sum(jnp.sum(terms, axis=0, keepdims=True), axis=1, keepdims=True)
    factor = lax.rsqrt(energy / (KV_ROWS * HALF) + eps)

    def to_new(s, q):
        return remote(
            new_out[s].at[q], new_in[s].at[pl.ds(b * SIDE, SIDE)], s4.at[s], r4.at[s], device(a, q)
        )

    def all_new(s):
        blocks = new_out[s].at[pl.ds(0, SIDE - 1)]
        return remote(blocks, blocks, s4.at[s], r4.at[s], device(*near[0]))

    for s in WAY_BACK:
        c, ts = TURNS[s]
        first, last = ends[ts[0]][0], ends[ts[-1]][1]
        raw = A_COEF * mat[c, first:last, :].astype(F32) + jnp.dot(
            poly[first:last, :], mat[c], preferred_element_type=F32
        )
        new = (raw * factor).astype(BF16)
        for q in range(SIDE):
            for n, t in enumerate(ts):
                rows_t = new[n * TOP:n * TOP + SIDE * TALLS[t], q * WIDE:(q + 1) * WIDE]
                new_out[s][q, :, n * TALLS[0]:n * TALLS[0] + TALLS[t], :] = rows_t.reshape(SIDE, TALLS[t], WIDE)
        for _, pb in b_peers:
            to_new(s, pb).start()
        new_in[s][pl.ds(b * SIDE, SIDE)] = new_out[s][b]

    def to_out(s, k):
        d = device(*peers[k])
        return remote(out_blocks[s].at[k], out_ref.at[piece(a, b, s)], s5.at[s], r5.at[s], d)

    def all_out(s, n):
        blocks = out_blocks[s].at[pl.ds(0, n)]
        return remote(blocks, blocks, s5.at[s], r5.at[s], device(*near[0]))

    for s in WAY_BACK:
        all_new(s).wait_recv()
        for k in range(DEVS):
            out_blocks[s][k] = new_in[s][place_at[k]]
            if k < DEVS - 1:
                to_out(s, k).start()
        pltpu.make_async_copy(out_blocks[s].at[DEVS - 1], out_ref.at[piece(a, b, s)], r5.at[s]).start()

    for n in range(2):
        swap(n).wait_send()
    for s in range(STAGES):
        all_sub(s, DEVS - 1).wait_send()
        all_mat(s).wait_send()
        all_new(s).wait_send()
    for s in range(STAGES):
        all_out(s, DEVS).wait_recv()
        all_out(s, DEVS - 1).wait_send()


def shards(iterate, block_matrix):
    dma = pltpu.SemaphoreType.DMA

    def buffers(lead):
        return [pltpu.VMEM((*lead(height(ts)), WIDE), BF16) for _, ts in TURNS]

    return pl.pallas_call(
        kernel,
        out_shape=pltpu.VMEM(iterate.shape, BF16),
        in_specs=[pl.BlockSpec(memory_space=pltpu.HBM), pl.BlockSpec(memory_space=pltpu.HBM)],
        out_specs=pl.BlockSpec(memory_space=pl.ANY),
        scratch_shapes=[
            pltpu.SMEM((DEVS,), jnp.int32),
            pltpu.VMEM((2, KV_ROWS, SIDE * WIDE), BF16),
            pltpu.VMEM((BLK, 10 * BLK), BF16),
            pltpu.VMEM((BLK, 10 * BLK), BF16),
            pltpu.VMEM((KV_ROWS, KV_ROWS), BF16),
            *buffers(lambda tall: (DEVS, tall)),
            *buffers(lambda tall: (SIDE, SIDE * tall)),
            *buffers(lambda tall: (SIDE, SIDE, tall)),
            *buffers(lambda tall: (DEVS, tall)),
            *buffers(lambda tall: (DEVS, tall)),
            dma((1,)), pltpu.SemaphoreType.REGULAR,
            dma((STAGES,)), dma((STAGES,)),
            dma((STAGES,)), dma((STAGES,)),
            dma((2,)), dma((2,)),
            dma((STAGES,)), dma((STAGES,)),
            dma((STAGES,)), dma((STAGES,)),
        ],
        compiler_params=pltpu.CompilerParams(
            collective_id=0, has_side_effects=True, vmem_limit_bytes=40 * 1024 * 1024
        ),
        cost_estimate=pl.CostEstimate(flops=1_900_000_000, bytes_accessed=4_194_304, transcendentals=0),
    )(
        pltpu.with_memory_space_constraint(block_matrix, pltpu.HBM),
        pltpu.with_memory_space_constraint(iterate, pltpu.HBM),
    )


def solution(mesh):
    return jax.shard_map(
        shards,
        mesh=mesh,
        in_specs=(P(("grp", "row"), None), P("grp")),
        out_specs=P(("grp", "row"), None),
        check_vma=False,
    )
```

```python
import jax
import jax.numpy as jnp
from jax import lax
from jax.experimental import pallas as pl
from jax.experimental.pallas import tpu as pltpu
from jax.sharding import PartitionSpec as P

BLK = 128
SIDE = 4
DEVS = SIDE * SIDE
SUB = 256
KV_ROWS = 512
HALF = 2048
WIDE = 128
TALLS = (64, 64)
TURNS = ((0, (0, 1)), (1, (0,)), (1, (1,)))
WAY_BACK = (1, 2, 0)
STAGES = len(TURNS)
TOP = SIDE * TALLS[0]
MESH = pl.DeviceIdType.MESH

A_COEF = 3.4445
B_COEF = -4.775
C_COEF = 2.0315
eps = 1e-06
F32 = jnp.float32
BF16 = jnp.bfloat16


def height(ts):
    return sum(TALLS[t] for t in ts)


def kernel(
    owner_hbm, x_ref, out_ref,
    owner_ref, mat, part_out, part_in, gram_ref, *refs,
):
    in_sub, in_sorted, new_out, new_in, out_blocks = (refs[i * STAGES:(i + 1) * STAGES] for i in range(5))
    local_sem, gate, s1, r1, s2, r2, s3, r3, s4, r4, s5, r5 = refs[5 * STAGES:]
    group = lax.axis_index("grp")
    me = lax.axis_index("row")
    turn = lax.rem(group, 2)
    y, x = me // SIDE, lax.rem(me, SIDE)
    a = y + turn * (x - y)
    b = x + turn * (y - x)
    step_a = SIDE - (SIDE - 1) * turn
    step_b = 1 + (SIDE - 1) * turn

    def device(a_, b_):
        return a_ * step_a + b_ * step_b

    def shift(v, d):
        return lax.rem(v + d, SIDE)

    a_peers = [(shift(a, d), b) for d in (2, 1, 3)]
    b_peers = [(a, shift(b, d)) for d in (2, 1, 3)]
    near = a_peers + b_peers
    far = [(shift(a, da), shift(b, db)) for da in (2, 1, 3) for db in (2, 1, 3)]
    peers = far + near

    def piece(a_, b_, s):
        c, ts = TURNS[s]
        return pl.ds(ts[0] * TALLS[0], height(ts)), pl.ds(pl.multiple_of((a_ * SIDE + b_) * SUB + c * WIDE, WIDE), WIDE)

    def rows(s):
        ts = TURNS[s][1]
        return pl.ds(ts[0] * TOP, SIDE * height(ts))

    def lanes(q):
        return pl.ds(pl.multiple_of(q * WIDE, WIDE), WIDE)

    def remote(src, dst, send, recv, peer):
        return pltpu.make_async_remote_copy(
            src_ref=src, dst_ref=dst, send_sem=send, recv_sem=recv,
            device_id=(group, peer), device_id_type=MESH,
        )

    fetch = pltpu.make_async_copy(owner_hbm, owner_ref, local_sem.at[0])
    barrier = pltpu.get_barrier_semaphore()
    for pa, pb in near:
        pl.semaphore_signal(barrier, inc=1, device_id=(group, device(pa, pb)), device_id_type=MESH)
    pl.semaphore_wait(barrier, len(near))
    for pa, pb in a_peers:
        pl.semaphore_signal(gate, inc=1, device_id=(group, device(pa, pb)), device_id_type=MESH)

    def to_sub(s, pa, pb):
        d = device(pa, pb)
        return remote(x_ref.at[piece(pa, pb, s)], in_sub[s].at[me], s1.at[s], r1.at[s], d)

    def all_sub(s, n):
        blocks = in_sub[s].at[pl.ds(0, n)]
        return remote(blocks, blocks, s1.at[s], r1.at[s], device(*near[0]))

    own = [
        pltpu.make_async_copy(x_ref.at[piece(a, b, s)], in_sub[s].at[me], r1.at[s])
        for s in range(STAGES)
    ]
    for pa, pb in near:
        to_sub(0, pa, pb).start()
    fetch.start()
    pl.semaphore_wait(gate, SIDE - 1)
    for pa, pb in far:
        to_sub(0, pa, pb).start()
    for s in range(STAGES):
        own[s].start()
        if s:
            for pa, pb in peers:
                to_sub(s, pa, pb).start()

    fetch.wait()
    owners = [owner_ref[r] for r in range(DEVS)]
    places = []
    for r in range(DEVS):
        p = owners[r] * SIDE
        for q in range(r):
            p = p + jnp.where(owners[q] == owners[r], 1, 0)
        places.append(p)
    order = []
    for k in range(DEVS):
        o = jnp.int32(0)
        for r in range(1, DEVS):
            o = o + jnp.where(places[r] == k, r, 0)
        order.append(o)

    def to_mat(s, m):
        return remote(
            in_sorted[s].at[m], mat.at[TURNS[s][0], rows(s), lanes(b)], s2.at[s], r2.at[s], device(a, m)
        )

    def all_mat(s):
        blocks = in_sorted[s].at[pl.ds(0, SIDE - 1)]
        return remote(blocks, blocks, s2.at[s], r2.at[s], device(*near[0]))

    for s in range(STAGES):
        all_sub(s, DEVS).wait_recv()
        for m in range(SIDE):
            for i in range(SIDE):
                block = in_sub[s][order[m * SIDE + i]]
                for n, t in enumerate(TURNS[s][1]):
                    tall = TALLS[t]
                    first = n * TOP + i * tall
                    in_sorted[s][m, first:first + tall, :] = block[n * TALLS[0]:n * TALLS[0] + tall]
        for _, pb in b_peers:
            to_mat(s, pb).start()
        mat[TURNS[s][0], rows(s), lanes(b)] = in_sorted[s][b]

    def arrive(s):
        all_mat(s).wait_recv()

    ends = ((0, TOP), (TOP, KV_ROWS))

    def product(c, i, k):
        return lax.dot_general(
            mat[c, ends[i][0]:ends[i][1], :], mat[c, ends[k][0]:ends[k][1], :],
            (((1,), (1,)), ((), ())), preferred_element_type=F32,
        )

    partner = device(a + 1 - 2 * lax.rem(a, 2), b)

    quads = ((0, 0), (0, 1), (1, 1))
    edge = TOP // BLK
    pairs = [(i, j) for i in range(SIDE) for j in range(i, SIDE)]
    blocks = [[p for p in pairs if p[1] < edge], [p for p in pairs if p[1] >= edge]]
    starts = [0, len(blocks[0])]

    def swap(n):
        span = pl.ds(starts[n] * BLK, len(blocks[n]) * BLK)
        return remote(part_out.at[:, span], part_in.at[:, span], s3.at[n], r3.at[n], partner)

    arrive(0)
    part = {quad: product(0, *quad) for quad in quads}
    mine = {}
    for n in range(2):
        arrive(1 + n)
        for quad in quads[:1] if n == 0 else quads[1:]:
            part[quad] = part[quad] + product(1, *quad)
        for k, (i, j) in enumerate(blocks[n]):
            quad = part[i // edge, j // edge]
            u, v = i % edge * BLK, j % edge * BLK
            mine[i, j] = quad[u:u + BLK, v:v + BLK]
            part_out[:, (starts[n] + k) * BLK:(starts[n] + k + 1) * BLK] = mine[i, j].astype(BF16)
        swap(n).start()
    for n in range(2):
        swap(n).wait_recv()
        for k, (i, j) in enumerate(blocks[n]):
            block = mine[i, j] + part_in[:, (starts[n] + k) * BLK:(starts[n] + k + 1) * BLK].astype(F32)
            gram_ref[i * BLK:(i + 1) * BLK, j * BLK:(j + 1) * BLK] = block.astype(BF16)
            if i != j:
                gram_ref[j * BLK:(j + 1) * BLK, i * BLK:(i + 1) * BLK] = block.T.astype(BF16)
    gram = gram_ref[...]
    square = jnp.dot(gram, gram, preferred_element_type=F32)
    gram32 = gram.astype(F32)
    poly = (B_COEF * gram32 + C_COEF * square).astype(BF16)
    poly32 = poly.astype(F32)

    turned = jnp.dot(poly, gram, preferred_element_type=F32)
    diagonal = lax.broadcasted_iota(jnp.int32, (KV_ROWS, KV_ROWS), 0) == lax.broadcasted_iota(
        jnp.int32, (KV_ROWS, KV_ROWS), 1
    )
    terms = (
        jnp.where(diagonal, (A_COEF * A_COEF) * gram32, 0.0)
        + (2 * A_COEF) * (poly32 * gram32)
        + turned * poly32
    )
    energy = jnp.sum(jnp.sum(terms, axis=0, keepdims=True), axis=1, keepdims=True)
    factor = lax.rsqrt(energy / (KV_ROWS * HALF) + eps)

    def to_new(s, q):
        return remote(
            new_out[s].at[q], new_in[s].at[pl.ds(b * SIDE, SIDE)], s4.at[s], r4.at[s], device(a, q)
        )

    def all_new(s):
        blocks = new_out[s].at[pl.ds(0, SIDE - 1)]
        return remote(blocks, blocks, s4.at[s], r4.at[s], device(*near[0]))

    for s in WAY_BACK:
        c, ts = TURNS[s]
        first, last = ends[ts[0]][0], ends[ts[-1]][1]
        raw = A_COEF * mat[c, first:last, :].astype(F32) + jnp.dot(
            poly[first:last, :], mat[c], preferred_element_type=F32
        )
        new = (raw * factor).astype(BF16)
        for q in range(SIDE):
            for n, t in enumerate(ts):
                rows_t = new[n * TOP:n * TOP + SIDE * TALLS[t], q * WIDE:(q + 1) * WIDE]
                new_out[s][q, :, n * TALLS[0]:n * TALLS[0] + TALLS[t], :] = rows_t.reshape(SIDE, TALLS[t], WIDE)
        for _, pb in b_peers:
            to_new(s, pb).start()
        new_in[s][pl.ds(b * SIDE, SIDE)] = new_out[s][b]

    def to_out(s, pa, pb):
        d = device(pa, pb)
        return remote(out_blocks[s].at[d], out_ref.at[piece(a, b, s)], s5.at[s], r5.at[s], d)

    def all_out(s, n):
        blocks = out_blocks[s].at[pl.ds(0, n)]
        return remote(blocks, blocks, s5.at[s], r5.at[s], device(*near[0]))

    for s in WAY_BACK:
        all_new(s).wait_recv()
        for r in range(DEVS):
            out_blocks[s][r] = new_in[s][places[r]]
        for pa, pb in peers:
            to_out(s, pa, pb).start()
        pltpu.make_async_copy(out_blocks[s].at[me], out_ref.at[piece(a, b, s)], r5.at[s]).start()

    for n in range(2):
        swap(n).wait_send()
    for s in range(STAGES):
        all_sub(s, DEVS - 1).wait_send()
        all_mat(s).wait_send()
        all_new(s).wait_send()
    for s in range(STAGES):
        all_out(s, DEVS).wait_recv()
        all_out(s, DEVS - 1).wait_send()


def shards(iterate, block_matrix):
    dma = pltpu.SemaphoreType.DMA

    def buffers(lead):
        return [pltpu.VMEM((*lead(height(ts)), WIDE), BF16) for _, ts in TURNS]

    return pl.pallas_call(
        kernel,
        out_shape=pltpu.VMEM(iterate.shape, BF16),
        in_specs=[pl.BlockSpec(memory_space=pltpu.HBM), pl.BlockSpec(memory_space=pltpu.HBM)],
        out_specs=pl.BlockSpec(memory_space=pl.ANY),
        scratch_shapes=[
            pltpu.SMEM((DEVS,), jnp.int32),
            pltpu.VMEM((2, KV_ROWS, SIDE * WIDE), BF16),
            pltpu.VMEM((BLK, 10 * BLK), BF16),
            pltpu.VMEM((BLK, 10 * BLK), BF16),
            pltpu.VMEM((KV_ROWS, KV_ROWS), BF16),
            *buffers(lambda tall: (DEVS, tall)),
            *buffers(lambda tall: (SIDE, SIDE * tall)),
            *buffers(lambda tall: (SIDE, SIDE, tall)),
            *buffers(lambda tall: (DEVS, tall)),
            *buffers(lambda tall: (DEVS, tall)),
            dma((1,)), pltpu.SemaphoreType.REGULAR,
            dma((STAGES,)), dma((STAGES,)),
            dma((STAGES,)), dma((STAGES,)),
            dma((2,)), dma((2,)),
            dma((STAGES,)), dma((STAGES,)),
            dma((STAGES,)), dma((STAGES,)),
        ],
        compiler_params=pltpu.CompilerParams(
            collective_id=0, has_side_effects=True, vmem_limit_bytes=40 * 1024 * 1024
        ),
        cost_estimate=pl.CostEstimate(flops=1_900_000_000, bytes_accessed=4_194_304, transcendentals=0),
    )(
        pltpu.with_memory_space_constraint(block_matrix, pltpu.HBM),
        pltpu.with_memory_space_constraint(iterate, pltpu.HBM),
    )


def solution(mesh):
    return jax.shard_map(
        shards,
        mesh=mesh,
        in_specs=(P(("grp", "row"), None), P("grp")),
        out_specs=P(("grp", "row"), None),
        check_vma=False,
    )
```
